128 devices in a mesh: inp: 4 (over z_lo, core), out: 4 (over x), dep: 8 (over y, z_hi).
Axes of the slice: x: 4, y: 4, z: 4 (z_hi: 2, z_lo: 2; z = z_hi * 2 + z_lo), core: 2. Of those that a mesh axis runs over, the one named last changes fastest.
Arguments:
- tokens: bfloat16 [512, 8192], P(('out', 'dep'), 'inp'), may hold values from -6 to 6
- cotangent: bfloat16 [512, 8192], P(('out', 'dep'), 'inp'), may hold values from -6 to 6
- gate_weight: bfloat16 [8192, 28672], P('inp', ('out', 'dep')), may hold values from -0.0625 to 0.0625
- up_weight: bfloat16 [8192, 28672], P('inp', ('out', 'dep')), may hold values from -0.0625 to 0.0625
- down_weight: bfloat16 [28672, 8192], P(('out', 'dep'), 'inp'), may hold values from -0.03125 to 0.03125
- seq_ids: int32 [512], P(('out', 'dep')), may hold values from 0 to 15, never falling along the last dimension, each value on 1 to 64 neighbouring positions
- chosen: int32 [512], P(('out', 'dep')), may hold values 0 or 1
- margins: float32 [16], replicated, may hold values from -3 to 3
- counts: int32 [32], replicated, may hold values from 32 to 256
Outputs:
- grad_input: bfloat16 [512, 8192], P(('out', 'dep'), 'inp')
- grad_gate: bfloat16 [8192, 28672], P('inp', ('out', 'dep'))
- grad_up: bfloat16 [8192, 28672], P('inp', ('out', 'dep'))
- grad_down: bfloat16 [28672, 8192], P(('out', 'dep'), 'inp')
The draws below stay inside these ranges and needn't reach their ends.
Inputs may be any that keep to these rules, and one draw needn't show every extreme that they name: `seq_ids`: a pair's tokens stand in one run; ids never fall along the tokens.
All inputs are finite; a program needn't handle non-finite values. No bound on the sum of `chosen` on one device may be relied on, other than what follows from the above.
Results may differ from the reference program's by a relative error of at most 0.0058.
Values may be sent and summed in bfloat16 or wider, within the bound.
A program may use at most 128 MiB of HBM per device.

```python
import math
import jax
import jax.numpy as jnp
import numpy as np

D = 8192
FF = 28672
TOKENS = 512
PAIRS = 16
SEQS = 32


def with_ends(entries, own_key, smallest, top_value):
    longest = entries.shape.index(max(entries.shape))
    spots = []
    for shift in (0, 1):
        where = [jax.random.randint(jax.random.fold_in(own_key, axis), (), 0, length) for axis, length in enumerate(entries.shape)]
        where[longest] = (where[longest] + shift) % entries.shape[longest]
        spots.append(tuple(where))
    return entries.at[spots[0]].set(smallest).at[spots[1]].set(top_value)


def steps_of(key, extent, split, smallest, high):
    level = 1.0
    for position, parts in split:
        steps = jax.random.uniform(jax.random.fold_in(jax.random.fold_in(key, 6), position), (parts,), jnp.float32, smallest / len(split), high / len(split))
        level = level * jnp.repeat(jnp.exp(steps), extent[position] // parts).reshape((-1,) + (1,) * (len(extent) - 1 - position))
    return level


def split_up(count, total, most, skew):
    loads = [(1 << 20) // math.isqrt(grade ** skew) + 1 for grade in range(2, count + 1)]
    rest, given = total - most - (count - 1), [1] * (count - 1)
    while rest > 0:
        candidates = [i for i in range(count - 1) if given[i] < most]
        pool, left = sum([loads[i] for i in candidates]), rest
        for i in candidates:
            more = min(most - given[i], max(1, left * loads[i] // pool), rest)
            given[i] = given[i] + more
            rest = rest - more
    return np.array([most] + given)


def uneven(own_key, number_of, total, reach, skew):
    if number_of == 2:
        one = jax.random.randint(own_key, (), max(1, total - reach), min(reach, total - 1) + 1)
        return jnp.stack([one, total - one])
    sizes = jnp.asarray(split_up(number_of, total, reach, skew), jnp.int32)
    twos = (number_of - 1) // 2
    donor, receiver = sizes[1:1 + 2 * twos:2], sizes[2:2 + 2 * twos:2]
    room = jnp.minimum(donor - 1, reach - receiver)
    shifted = jax.random.randint(jax.random.fold_in(own_key, 1), (twos,), 0, 1 << 20) % (room + 1)
    sizes = sizes.at[1:1 + 2 * twos:2].set(donor - shifted).at[2:2 + 2 * twos:2].set(receiver + shifted)
    return sizes[jax.random.permutation(jax.random.fold_in(own_key, 2), number_of)]


def centred(rng, shape, width, most, shards=(), dtype=jnp.bfloat16):
    result = jax.random.normal(rng, shape, jnp.float32) * width
    if len(shards) > 0:
        result = steps_of(rng, shape, shards, -0.22, 0.18) * result
    return jnp.clip(result, min=-most, max=most).astype(dtype)


def setup_inputs(seed: int = 0) -> dict:
    arg_keys = jax.random.split(jax.random.key(seed), 10)
    return {
        "tokens": centred(arg_keys[0], (TOKENS, D), 1.0, 6.0, ((0, 32), (1, 4))),
        "cotangent": centred(arg_keys[1], (TOKENS, D), 1.0, 6.0, ((0, 32), (1, 4))),
        "gate_weight": centred(arg_keys[2], (D, FF), D ** -0.5, 0.0625, ((0, 4), (1, 32))),
        "up_weight": centred(arg_keys[3], (D, FF), D ** -0.5, 0.0625, ((0, 4), (1, 32))),
        "down_weight": centred(arg_keys[4], (FF, D), FF ** -0.5, 0.03125, ((0, 32), (1, 4))),
        "seq_ids": jnp.searchsorted(jnp.cumsum(uneven(arg_keys[5], PAIRS, TOKENS, min(TOKENS // 2, 64), 1)), jnp.arange(TOKENS), side="right").astype(jnp.int32),
        "chosen": with_ends((jax.random.randint(arg_keys[6], (TOKENS,), 0, 2) < 1).astype(jnp.int32), jax.random.fold_in(arg_keys[6], 1), 0, 1),
        "margins": jnp.clip(jax.random.uniform(arg_keys[7], (PAIRS,), jnp.float32, -3.0, 3.0), -3.0, 3.0),
        "counts": with_ends(jax.random.randint(arg_keys[8], (SEQS,), 32, 257), jax.random.fold_in(arg_keys[8], 1), 32, 256).astype(jnp.int32),
    }


SIMPO_BETA = 2.5
LOSS_SCALE = 64.0


def reference(tokens, cotangent, gate_weight, up_weight, down_weight, seq_ids, chosen, margins, counts):
    pair_margin = margins[seq_ids]
    seq_length = counts[(2 * seq_ids + chosen).astype(jnp.int32)].astype(jnp.float32)
    polarity = 1.0 - 2.0 * chosen.astype(jnp.float32)
    token_weight = polarity * SIMPO_BETA * LOSS_SCALE * jax.nn.sigmoid(-pair_margin) / seq_length
    out_grad = (cotangent.astype(jnp.float32) * token_weight[:, None]).astype(jnp.bfloat16)
    gate_sum = jnp.dot(tokens, gate_weight, preferred_element_type=jnp.float32)
    up_sum = jnp.dot(tokens, up_weight, preferred_element_type=jnp.float32)
    logistic = jax.nn.sigmoid(gate_sum)
    swish = gate_sum * logistic
    hidden = (swish * up_sum).astype(jnp.bfloat16)
    hidden_grad = jnp.dot(out_grad, down_weight.T, preferred_element_type=jnp.float32)
    gate_grad = (hidden_grad * up_sum * logistic * (1.0 + gate_sum * (1.0 - logistic))).astype(jnp.bfloat16)
    up_grad = (hidden_grad * swish).astype(jnp.bfloat16)
    grad_input = jnp.dot(gate_grad, gate_weight.T, preferred_element_type=jnp.float32)
    grad_input = grad_input + jnp.dot(up_grad, up_weight.T, preferred_element_type=jnp.float32)
    grad_gate = jnp.dot(tokens.T, gate_grad, preferred_element_type=jnp.float32)
    grad_up = jnp.dot(tokens.T, up_grad, preferred_element_type=jnp.float32)
    grad_down = jnp.dot(hidden.T, out_grad, preferred_element_type=jnp.float32)
    return (grad_input.astype(jnp.bfloat16), grad_gate.astype(jnp.bfloat16),
            grad_up.astype(jnp.bfloat16), grad_down.astype(jnp.bfloat16))
```

```python
import jax
import jax.numpy as jnp
from jax import lax
from jax.experimental import pallas as pl
from jax.experimental.pallas import tpu as pltpu
from jax.sharding import PartitionSpec as P

SIMPO_BETA = 2.5
LOSS_SCALE = 64.0
MESH = pl.DeviceIdType.MESH
BF16 = jnp.bfloat16
F32 = jnp.float32

WIDTH = 2048
HALF = 1024
UNITS = 896
ROWS = 16
CHUNK = 256
OWN = 128


def dot(left, right, dims):
    return lax.dot_general(left, right, (dims, ((), ())), preferred_element_type=F32)


def kernel(
    tok_ref,
    cot_ref,
    gate_ref,
    up_ref,
    down_ref,
    seq_ref,
    chosen_ref,
    margin_ref,
    count_ref,
    gin_ref,
    ggate_ref,
    gup_ref,
    gdown_ref,
    wgu,
    wdn,
    tok,
    og,
    ogown,
    part,
    xs,
    xr,
    summed,
    zs,
    zr,
    hid,
    gug,
    gpart,
    ra1,
    rb1,
    sa,
    sb,
    r2,
    fin,
    hsrc,
    hdst,
    wsem,
    hsem_s,
    hsem_r,
    ag_s,
    ag_r,
    x_s,
    x_r,
    z_s,
    z_r,
    c_s,
    c_r,
    rs_s,
    rs_r,
    f_s,
    f_r,
):
    inp, x, dep = lax.axis_index("inp"), lax.axis_index("out"), lax.axis_index("dep")
    zl, core = inp // 2, inp % 2
    y, zh = dep // 2, dep % 2
    at_x = lambda d: (inp, (x + d) % 4, dep)
    at_y = lambda d: (inp, x, ((y + d) % 4) * 2 + zh)
    at_zh = (inp, x, y * 2 + 1 - zh)
    at_core = (zl * 2 + 1 - core, x, dep)
    at_zl = ((1 - zl) * 2 + core, x, dep)

    loads = [
        pltpu.make_async_copy(gate_ref, wgu.at[:, pl.ds(0, UNITS)], wsem.at[0]),
        pltpu.make_async_copy(up_ref, wgu.at[:, pl.ds(UNITS, UNITS)], wsem.at[1]),
        pltpu.make_async_copy(down_ref, wdn, wsem.at[2]),
    ]
    for cp in loads:
        cp.start()

    barrier = pltpu.get_barrier_semaphore()
    greeted = [at_x(1), at_x(2), at_x(3), at_y(1), at_y(2), at_y(3), at_zh, at_core, at_zl]
    for who in greeted:
        pl.semaphore_signal(barrier, inc=1, device_id=who, device_id_type=MESH)

    sent = []

    def send(src, dst, s_sem, r_sem, who):
        cp = pltpu.make_async_remote_copy(
            src_ref=src, dst_ref=dst, send_sem=s_sem, recv_sem=r_sem, device_id=who, device_id_type=MESH
        )
        cp.start()
        sent.append(cp)
        return cp

    tok[0, x, y] = tok_ref[...]
    row = lax.broadcasted_iota(jnp.int32, (ROWS, 128), 0)
    margin = jnp.zeros((ROWS, 128), F32)
    length = jnp.ones((ROWS, 128), F32)
    polarity = jnp.zeros((ROWS, 128), F32)
    for t in range(ROWS):
        pair, pick = seq_ref[t], chosen_ref[t]
        margin = jnp.where(row == t, margin_ref[pair], margin)
        length = jnp.where(row == t, count_ref[2 * pair + pick].astype(F32), length)
        polarity = jnp.where(row == t, 1.0 - 2.0 * pick.astype(F32), polarity)
    weight = polarity * SIMPO_BETA * LOSS_SCALE * jax.nn.sigmoid(-margin) / length
    for j in range(WIDTH // 128):
        cols = pl.ds(j * 128, 128)
        value = (cot_ref[:, cols].astype(F32) * weight).astype(BF16)
        ogown[:, cols] = value
        og[0, x, y, :, cols] = value

    pl.semaphore_wait(barrier, len(greeted))

    bufs = (tok, og)
    cols_of = (pl.ds(0, HALF), pl.ds(HALF, HALF))

    def ag1(a, s):
        got = []
        for h in range(2):
            for d in range(1, 4):
                spot = bufs[a].at[s, x, y, :, cols_of[h]]
                who = at_y(d) if h == 0 else at_x(d)
                got.append(send(spot, spot, ag_s.at[a, s, h, 0, d - 1], ag_r.at[a, s, h, 0, d - 1], who))
        return got

    def ag2(a, s):
        got = []
        for h in range(2):
            for d in range(1, 4):
                if h == 0:
                    spot, who = bufs[a].at[s, x, :, :, cols_of[h]], at_x(d)
                else:
                    spot, who = bufs[a].at[s, :, y, :, cols_of[h]], at_y(d)
                got.append(send(spot, spot, ag_s.at[a, s, h, 1, d - 1], ag_r.at[a, s, h, 1, d - 1], who))
        return got

    def arrived(cps):
        for cp in cps:
            cp.wait_recv()

    t01 = ag1(0, 0)
    hops = [
        send(tok_ref, tok.at[1, x, y], hsem_s.at[0], hsem_r.at[0], at_zh),
        send(ogown, og.at[1, x, y], hsem_s.at[1], hsem_r.at[1], at_zh),
    ]
    o01 = ag1(1, 0)
    arrived(t01)
    t02 = ag2(0, 0)
    arrived(hops)
    t11 = ag1(0, 1)
    o11 = ag1(1, 1)
    arrived(o01)

    mine = pl.ds(pl.multiple_of(core * OWN, OWN), OWN)
    other = pl.ds(pl.multiple_of((1 - core) * OWN, OWN), OWN)

    def piece_cols(p):
        return pl.ds(p * UNITS, UNITS)

    def multiply(s, p):
        if p < 2:
            part[p] = dot(tok[s].reshape(CHUNK, WIDTH), wgu[:, piece_cols(p)], ((1,), (0,)))
        else:
            part[p] = dot(og[s].reshape(CHUNK, WIDTH), wdn[...], ((1,), (1,)))
        xs[s, p] = part[p, other].astype(BF16)
        return send(xs.at[s, p], xr.at[s, p], x_s.at[s, p], x_r.at[s, p], at_core)

    def pair_sum(s, p, cp):
        cp.wait_recv()
        total = part[p, mine] + xr[s, p].astype(F32)
        summed[s, p] = total
        zs[s, p] = total.astype(BF16)
        return send(zs.at[s, p], zr.at[s, p], z_s.at[s, p], z_r.at[s, p], at_zl)

    zcp = {}

    def gate_up(s):
        first = multiply(s, 0)
        second = multiply(s, 1)
        zcp[s, 0] = pair_sum(s, 0, first)
        zcp[s, 1] = pair_sum(s, 1, second)

    def hidden_grad(s):
        third = multiply(s, 2)
        zcp[s, 2] = pair_sum(s, 2, third)

    loads[0].wait()
    loads[1].wait()
    arrived(t02)
    o02 = ag2(1, 0)
    gate_up(0)
    arrived(t11)
    arrived(o02)
    t12 = ag2(0, 1)
    loads[2].wait()
    hidden_grad(0)
    arrived(o11)
    arrived(t12)
    o12 = ag2(1, 1)
    gate_up(1)
    arrived(o12)
    hidden_grad(1)

    def activate(s):
        for p in range(3):
            zcp[s, p].wait_recv()

        def rows16(i, carry):
            rows = pl.ds(pl.multiple_of(i * 16, 16), 16)
            gate_sum = summed[s, 0, rows] + zr[s, 0, rows].astype(F32)
            up_sum = summed[s, 1, rows] + zr[s, 1, rows].astype(F32)
            hg = summed[s, 2, rows] + zr[s, 2, rows].astype(F32)
            logistic = jax.nn.sigmoid(gate_sum)
            swish = gate_sum * logistic
            at = pl.ds(pl.multiple_of(core * OWN + i * 16, 16), 16)
            gug[s, at, pl.ds(0, UNITS)] = (
                hg * up_sum * logistic * (1.0 + gate_sum * (1.0 - logistic))
            ).astype(BF16)
            gug[s, at, pl.ds(UNITS, UNITS)] = (hg * swish).astype(BF16)
            hid[s, at] = (swish * up_sum).astype(BF16)
            return carry

        lax.fori_loop(0, OWN // 16, rows16, 0)
        return [
            send(gug.at[s, mine], gug.at[s, mine], c_s.at[s, 0], c_r.at[s, 0], at_core),
            send(hid.at[s, mine], hid.at[s, mine], c_s.at[s, 1], c_r.at[s, 1], at_core),
        ]

    def grad_in(s):
        got = []
        for h in range(2):
            for q in range(2):
                cols = pl.ds(h * HALF + q * 512, 512)
                value = dot(gug[s], wgu[cols, :], ((1,), (1,))).astype(BF16)
                gpart[s, :, :, :, cols] = value.reshape(4, 4, ROWS, 512)
            for d in range(1, 4):
                if h == 0:
                    src, dst, who = gpart.at[s, (x + d) % 4, :, :, cols_of[0]], ra1.at[s, d - 1], at_x(d)
                else:
                    src, dst, who = gpart.at[s, :, (y + d) % 4, :, cols_of[1]], rb1.at[s, d - 1], at_y(d)
                got.append(send(src, dst, rs_s.at[s, h, 0, d - 1], rs_r.at[s, h, 0, d - 1], who))
        return got

    def scatter2(s, cps):
        arrived(cps)
        got = []
        total = gpart[s, x, :, :, cols_of[0]].astype(F32)
        for d in range(3):
            total += ra1[s, d].astype(F32)
        sa[s] = total.astype(BF16)
        total = gpart[s, :, y, :, cols_of[1]].astype(F32)
        for d in range(3):
            total += rb1[s, d].astype(F32)
        sb[s] = total.astype(BF16)
        for d in range(1, 4):
            got.append(
                send(sa.at[s, (y + d) % 4], r2.at[s, 0, d - 1], rs_s.at[s, 0, 1, d - 1], rs_r.at[s, 0, 1, d - 1], at_y(d))
            )
            got.append(
                send(sb.at[s, (x + d) % 4], r2.at[s, 1, d - 1], rs_s.at[s, 1, 1, d - 1], rs_r.at[s, 1, 1, d - 1], at_x(d))
            )
        return got

    def scatter_sum(s, cps):
        arrived(cps)
        a, b = sa[s, y].astype(F32), sb[s, x].astype(F32)
        for d in range(3):
            a += r2[s, 0, d].astype(F32)
            b += r2[s, 1, d].astype(F32)
        return a, b

    ccp = activate(0)
    arrived(ccp)
    g0 = grad_in(0)
    p0 = scatter2(0, g0)
    ccp = activate(1)
    arrived(ccp)
    g1 = grad_in(1)
    a, b = scatter_sum(0, p0)
    fin[:, cols_of[0]] = a
    fin[:, cols_of[1]] = b

    def gate_tile(i, carry):
        rows = pl.ds(pl.multiple_of(i * 256, 256), 256)
        left = tok[:, :, :, :, rows].reshape(2 * CHUNK, 256)
        value = dot(left, gug[...].reshape(2 * CHUNK, 2 * UNITS), ((0,), (0,)))
        ggate_ref[rows, :] = value[:, :UNITS].astype(BF16)
        gup_ref[rows, :] = value[:, UNITS:].astype(BF16)
        return carry

    lax.fori_loop(0, WIDTH // 256, gate_tile, 0)
    p1 = scatter2(1, g1)

    def down_tile(i, carry):
        rows = pl.ds(pl.multiple_of(i * 128, 128), 128)
        left = hid[:, :, rows].reshape(2 * CHUNK, 128)
        value = dot(left, og[...].reshape(2 * CHUNK, WIDTH), ((0,), (0,)))
        gdown_ref[rows, :] = value.astype(BF16)
        return carry

    lax.fori_loop(0, UNITS // 128, down_tile, 0)
    a, b = scatter_sum(1, p1)
    hsrc[:, cols_of[0]] = a.astype(BF16)
    hsrc[:, cols_of[1]] = b.astype(BF16)
    last = send(hsrc, hdst, f_s.at[0], f_r.at[0], at_zh)
    last.wait_recv()
    gin_ref[...] = (fin[...] + hdst[...].astype(F32)).astype(BF16)
    for cp in sent:
        cp.wait_send()


def on_device(tokens, cotangent, gate_weight, up_weight, down_weight, seq_ids, chosen, margins, counts):
    vmem = pl.BlockSpec(memory_space=pltpu.VMEM)
    smem = pl.BlockSpec(memory_space=pltpu.SMEM)
    hbm = pl.BlockSpec(memory_space=pl.ANY)
    dma = pltpu.SemaphoreType.DMA
    return pl.pallas_call(
        kernel,
        out_shape=(
            jax.ShapeDtypeStruct((ROWS, WIDTH), BF16),
            jax.ShapeDtypeStruct((WIDTH, UNITS), BF16),
            jax.ShapeDtypeStruct((WIDTH, UNITS), BF16),
            jax.ShapeDtypeStruct((UNITS, WIDTH), BF16),
        ),
        in_specs=[vmem, vmem, hbm, hbm, hbm, smem, smem, smem, smem],
        out_specs=(vmem, vmem, vmem, vmem),
        scratch_shapes=[
            pltpu.VMEM((WIDTH, 2 * UNITS), BF16),
            pltpu.VMEM((UNITS, WIDTH), BF16),
            pltpu.VMEM((2, 4, 4, ROWS, WIDTH), BF16),
            pltpu.VMEM((2, 4, 4, ROWS, WIDTH), BF16),
            pltpu.VMEM((ROWS, WIDTH), BF16),
            pltpu.VMEM((3, CHUNK, UNITS), F32),
            pltpu.VMEM((2, 3, OWN, UNITS), BF16),
            pltpu.VMEM((2, 3, OWN, UNITS), BF16),
            pltpu.VMEM((2, 3, OWN, UNITS), F32),
            pltpu.VMEM((2, 3, OWN, UNITS), BF16),
            pltpu.VMEM((2, 3, OWN, UNITS), BF16),
            pltpu.VMEM((2, CHUNK, UNITS), BF16),
            pltpu.VMEM((2, CHUNK, 2 * UNITS), BF16),
            pltpu.VMEM((2, 4, 4, ROWS, WIDTH), BF16),
            pltpu.VMEM((2, 3, 4, ROWS, HALF), BF16),
            pltpu.VMEM((2, 3, 4, ROWS, HALF), BF16),
            pltpu.VMEM((2, 4, ROWS, HALF), BF16),
            pltpu.VMEM((2, 4, ROWS, HALF), BF16),
            pltpu.VMEM((2, 2, 3, ROWS, HALF), BF16),
            pltpu.VMEM((ROWS, WIDTH), F32),
            pltpu.VMEM((ROWS, WIDTH), BF16),
            pltpu.VMEM((ROWS, WIDTH), BF16),
            dma((3,)),
            dma((2,)),
            dma((2,)),
            dma((2, 2, 2, 2, 3)),
            dma((2, 2, 2, 2, 3)),
            dma((2, 3)),
            dma((2, 3)),
            dma((2, 3)),
            dma((2, 3)),
            dma((2, 2)),
            dma((2, 2)),
            dma((2, 2, 2, 3)),
            dma((2, 2, 2, 3)),
            dma((1,)),
            dma((1,)),
        ],
        compiler_params=pltpu.CompilerParams(
            collective_id=0, has_side_effects=True, vmem_limit_bytes=60 << 20
        ),
        cost_estimate=pl.CostEstimate(flops=15_000_000_000, bytes_accessed=22_000_000, transcendentals=0),
        name="simpo_backward",
    )(tokens, cotangent, gate_weight, up_weight, down_weight, seq_ids, chosen, margins, counts)


def solution(mesh):
    return jax.shard_map(
        on_device,
        mesh=mesh,
        in_specs=(
            P(("out", "dep"), "inp"),
            P(("out", "dep"), "inp"),
            P("inp", ("out", "dep")),
            P("inp", ("out", "dep")),
            P(("out", "dep"), "inp"),
            P(("out", "dep")),
            P(("out", "dep")),
            P(),
            P(),
        ),
        out_specs=(
            P(("out", "dep"), "inp"),
            P("inp", ("out", "dep")),
            P("inp", ("out", "dep")),
            P(("out", "dep"), "inp"),
        ),
        check_vma=False,
    )
```

```python
import jax
import jax.numpy as jnp
from jax import lax
from jax.experimental import pallas as pl
from jax.experimental.pallas import tpu as pltpu
from jax.sharding import PartitionSpec as P

SIMPO_BETA = 2.5
LOSS_SCALE = 64.0
MESH = pl.DeviceIdType.MESH
BF16 = jnp.bfloat16
F32 = jnp.float32

WIDTH = 2048
HALF = 1024
UNITS = 896
ROWS = 16
CHUNK = 256
OWN = 128
PIECES = (((0, 512), (512, 384)), ((0, UNITS),))


def dot(left, right, dims):
    return lax.dot_general(left, right, (dims, ((), ())), preferred_element_type=F32)


def kernel(
    tok_ref,
    cot_ref,
    gate_ref,
    up_ref,
    down_ref,
    seq_ref,
    chosen_ref,
    margin_ref,
    count_ref,
    gin_ref,
    ggate_ref,
    gup_ref,
    gdown_ref,
    wgate,
    wup,
    wdn,
    tok,
    og,
    cot,
    ogown,
    part,
    xs,
    xr,
    summed,
    zs,
    zr,
    slope,
    swished,
    hid,
    gug,
    gacc,
    gpart,
    ra1,
    rb1,
    sa,
    sb,
    r2,
    sa1,
    sb1,
    r21,
    fin,
    hsrc,
    hdst,
    lsem,
    hsem_s,
    hsem_r,
    ag_s,
    ag_r,
    x_s,
    x_r,
    z_s,
    z_r,
    c_s,
    c_r,
    k_s,
    k_r,
    rs_s,
    rs_r,
    f_s,
    f_r,
):
    inp, x, dep = lax.axis_index("inp"), lax.axis_index("out"), lax.axis_index("dep")
    zl, core = inp // 2, inp % 2
    y, zh = dep // 2, dep % 2
    at_x = lambda d: (inp, (x + d) % 4, dep)
    at_y = lambda d: (inp, x, ((y + d) % 4) * 2 + zh)
    at_zh = (inp, x, y * 2 + 1 - zh)
    at_core = (zl * 2 + 1 - core, x, dep)
    at_zl = ((1 - zl) * 2 + core, x, dep)

    barrier = pltpu.get_barrier_semaphore()
    greeted = [at_x(1), at_x(2), at_x(3), at_y(1), at_y(2), at_y(3), at_zh, at_core, at_zl]
    for who in greeted:
        pl.semaphore_signal(barrier, inc=1, device_id=who, device_id_type=MESH)

    def load(src, dst, i):
        cp = pltpu.make_async_copy(src, dst, lsem.at[i])
        cp.start()
        return cp

    cot_load = load(cot_ref, cot, 0)
    tok_load = load(tok_ref, tok.at[0, x, y], 1)
    gate_load = load(gate_ref, wgate, 2)
    up_load = load(up_ref, wup, 3)
    down_load = load(down_ref, wdn, 4)

    sent = []

    def send(src, dst, s_sem, r_sem, who):
        cp = pltpu.make_async_remote_copy(
            src_ref=src, dst_ref=dst, send_sem=s_sem, recv_sem=r_sem, device_id=who, device_id_type=MESH
        )
        cp.start()
        sent.append(cp)
        return cp

    def arrived(cps):
        for cp in cps:
            cp.wait_recv()

    bufs = (tok, og)
    cols_of = (pl.ds(0, HALF), pl.ds(HALF, HALF))

    def ag1(a, s, own=None):
        got = []
        for d in range(1, 4):
            for h in range(2):
                spot = bufs[a].at[s, x, y, :, cols_of[h]]
                src = spot if own is None else own.at[:, cols_of[h]]
                who = at_y(d) if h == 0 else at_x(d)
                got.append(send(src, spot, ag_s.at[a, s, h, 0, d - 1], ag_r.at[a, s, h, 0, d - 1], who))
        return got

    def ag2(a, s):
        got = []
        for d in range(1, 4):
            for h in range(2):
                if h == 0:
                    spot, who = bufs[a].at[s, x, :, :, cols_of[h]], at_x(d)
                else:
                    spot, who = bufs[a].at[s, :, y, :, cols_of[h]], at_y(d)
                got.append(send(spot, spot, ag_s.at[a, s, h, 1, d - 1], ag_r.at[a, s, h, 1, d - 1], who))
        return got

    pl.semaphore_wait(barrier, len(greeted))
    t01 = ag1(0, 0, tok_ref)
    tok_hop = send(tok_ref, tok.at[1, x, y], hsem_s.at[0], hsem_r.at[0], at_zh)

    row = lax.broadcasted_iota(jnp.int32, (ROWS, 128), 0)
    margin = jnp.zeros((ROWS, 128), F32)
    length = jnp.ones((ROWS, 128), F32)
    polarity = jnp.zeros((ROWS, 128), F32)
    for t in range(ROWS):
        pair, pick = seq_ref[t], chosen_ref[t]
        margin = jnp.where(row == t, margin_ref[pair], margin)
        length = jnp.where(row == t, count_ref[2 * pair + pick].astype(F32), length)
        polarity = jnp.where(row == t, 1.0 - 2.0 * pick.astype(F32), polarity)
    weight = polarity * SIMPO_BETA * LOSS_SCALE * jax.nn.sigmoid(-margin) / length
    cot_load.wait()
    for j in range(WIDTH // 128):
        cols = pl.ds(j * 128, 128)
        value = (cot[:, cols].astype(F32) * weight).astype(BF16)
        ogown[:, cols] = value
        og[0, x, y, :, cols] = value
    og_hop = send(ogown, og.at[1, x, y], hsem_s.at[1], hsem_r.at[1], at_zh)

    tok_load.wait()
    arrived(t01)
    t02 = ag2(0, 0)
    arrived([tok_hop])
    t11 = ag1(0, 1)

    mine = pl.ds(pl.multiple_of(core * OWN, OWN), OWN)
    other = pl.ds(pl.multiple_of((1 - core) * OWN, OWN), OWN)

    def multiply(s, p):
        if p == 0:
            part[p] = dot(tok[s].reshape(CHUNK, WIDTH), wgate[...], ((1,), (0,)))
        elif p == 1:
            part[p] = dot(tok[s].reshape(CHUNK, WIDTH), wup[...], ((1,), (0,)))
        else:
            part[p] = dot(og[s].reshape(CHUNK, WIDTH), wdn[...], ((1,), (1,)))
        xs[s, p] = part[p, other].astype(BF16)
        return send(xs.at[s, p], xr.at[s, p], x_s.at[s, p], x_r.at[s, p], at_core)

    zcp = {}

    def pair_sum(s, p, cp, pieces=((0, UNITS),)):
        cp.wait_recv()
        total = part[p, mine] + xr[s, p].astype(F32)
        summed[s, p] = total
        zs[s, p] = total.astype(BF16)
        for k, (first, count) in enumerate(pieces):
            cols = pl.ds(first, count)
            zcp[s, p, k] = send(
                zs.at[s, p, :, cols], zr.at[s, p, :, cols], z_s.at[s, p, k], z_r.at[s, p, k], at_zl
            )

    def gate_up(s):
        first = multiply(s, 0)
        second = multiply(s, 1)
        pair_sum(s, 0, first)
        pair_sum(s, 1, second)

    def hidden_grad(s):
        pair_sum(s, 2, multiply(s, 2), PIECES[s])

    def by_rows(body):
        lax.fori_loop(0, OWN // 16, lambda i, c: (body(pl.multiple_of(i * 16, 16)), c)[1], 0)

    def activate(s):
        zcp[s, 0, 0].wait_recv()
        zcp[s, 1, 0].wait_recv()

        def body(i):
            rows = pl.ds(i, 16)
            gate_sum = summed[s, 0, rows] + zr[s, 0, rows].astype(F32)
            up_sum = summed[s, 1, rows] + zr[s, 1, rows].astype(F32)
            logistic = jax.nn.sigmoid(gate_sum)
            swish = gate_sum * logistic
            slope[s, rows] = up_sum * logistic * (1.0 + gate_sum * (1.0 - logistic))
            swished[s, rows] = swish
            hid[s, pl.ds(pl.multiple_of(core * OWN + i, 16), 16)] = (swish * up_sum).astype(BF16)

        by_rows(body)
        return send(hid.at[s, mine], hid.at[s, mine], c_s.at[s], c_r.at[s], at_core)

    def act_grad(s, k):
        zcp[s, 2, k].wait_recv()
        cols = pl.ds(*PIECES[s][k])

        def body(i):
            rows = pl.ds(i, 16)
            at = pl.ds(pl.multiple_of(core * OWN + i, 16), 16)
            hg = summed[s, 2, rows, cols] + zr[s, 2, rows, cols].astype(F32)
            gug[s, 0, at, cols] = (hg * slope[s, rows, cols]).astype(BF16)
            gug[s, 1, at, cols] = (hg * swished[s, rows, cols]).astype(BF16)

        by_rows(body)
        spot = gug.at[s, :, mine, cols]
        return send(spot, spot, k_s.at[s, k], k_r.at[s, k], at_core)

    def grad_in(s, ccps):
        got = []
        last = len(ccps) - 1
        for k, cp in enumerate(ccps):
            cp.wait_recv()
            cols = pl.ds(*PIECES[s][k])
            for h in range(2):
                for q in range(2):
                    wide = pl.ds(h * HALF + q * 512, 512)
                    value = dot(gug[s, 0, :, cols], wgate[wide, cols], ((1,), (1,)))
                    value += dot(gug[s, 1, :, cols], wup[wide, cols], ((1,), (1,)))
                    if k > 0:
                        value += gacc[:, wide]
                    if k < last:
                        gacc[:, wide] = value
                    else:
                        gpart[s, :, :, :, wide] = value.astype(BF16).reshape(4, 4, ROWS, 512)
                if k < last:
                    continue
                for d in range(1, 4):
                    if h == 0:
                        src, dst, who = gpart.at[s, (x + d) % 4, :, :, cols_of[0]], ra1.at[s, d - 1], at_x(d)
                    else:
                        src, dst, who = gpart.at[s, :, (y + d) % 4, :, cols_of[1]], rb1.at[s, d - 1], at_y(d)
                    got.append(send(src, dst, rs_s.at[s, h, 0, d - 1], rs_r.at[s, h, 0, d - 1], who))
        return got

    def scatter2(s, cps):
        arrived(cps)
        at_a, at_b, to, kind = ((sa, sb, r2, BF16), (sa1, sb1, r21, F32))[s]
        total = gpart[s, x, :, :, cols_of[0]].astype(F32)
        for d in range(3):
            total += ra1[s, d].astype(F32)
        at_a[...] = total.astype(kind)
        total = gpart[s, :, y, :, cols_of[1]].astype(F32)
        for d in range(3):
            total += rb1[s, d].astype(F32)
        at_b[...] = total.astype(kind)
        got = []
        for d in range(1, 4):
            got.append(
                send(at_a.at[(y + d) % 4], to.at[0, d - 1], rs_s.at[s, 0, 1, d - 1], rs_r.at[s, 0, 1, d - 1], at_y(d))
            )
            got.append(
                send(at_b.at[(x + d) % 4], to.at[1, d - 1], rs_s.at[s, 1, 1, d - 1], rs_r.at[s, 1, 1, d - 1], at_x(d))
            )
        return got

    def scatter_sum(s, cps, out):
        arrived(cps)
        at_a, at_b, to = ((sa, sb, r2), (sa1, sb1, r21))[s]
        for h, own in enumerate((at_a[y], at_b[x])):
            total = own.astype(F32)
            for d in range(3):
                total += to[h, d].astype(F32)
            out[:, cols_of[h]] = total

    arrived(t02)
    arrived(t11)
    t12 = ag2(0, 1)
    arrived([og_hop])
    o11 = ag1(1, 1)
    o01 = ag1(1, 0, ogown)
    gate_load.wait()
    up_load.wait()
    gate_up(0)
    arrived(t12)
    arrived(o11)
    o12 = ag2(1, 1)
    gate_up(1)
    arrived(o12)
    arrived(o01)
    o02 = ag2(1, 0)
    down_load.wait()
    hidden_grad(1)
    hid0 = activate(0)
    arrived(o02)
    hidden_grad(0)
    hid1 = activate(1)
    arrived([hid0, hid1])

    def down_tile(i, carry):
        rows = pl.ds(pl.multiple_of(i * 128, 128), 128)
        left = hid[:, :, rows].reshape(2 * CHUNK, 128)
        value = dot(left, og[...].reshape(2 * CHUNK, WIDTH), ((0,), (0,)))
        gdown_ref[rows, :] = value.astype(BF16)
        return carry

    lax.fori_loop(0, UNITS // 128, down_tile, 0)
    cc1 = [act_grad(1, k) for k in range(len(PIECES[1]))]
    g1 = grad_in(1, cc1)
    cc0 = [act_grad(0, k) for k in range(len(PIECES[0]))]
    g0 = grad_in(0, cc0)

    def gate_tile(i, carry):
        rows = pl.ds(pl.multiple_of(i * 256, 256), 256)
        left = tok[:, :, :, :, rows].reshape(2 * CHUNK, 256)
        right = jnp.concatenate(
            [gug[:, 0].reshape(2 * CHUNK, UNITS), gug[:, 1].reshape(2 * CHUNK, UNITS)], axis=1
        )
        value = dot(left, right, ((0,), (0,)))
        ggate_ref[rows, :] = value[:, :UNITS].astype(BF16)
        gup_ref[rows, :] = value[:, UNITS:].astype(BF16)
        return carry

    lax.fori_loop(0, 4, gate_tile, 0)
    p1 = scatter2(1, g1)
    lax.fori_loop(4, 8, gate_tile, 0)
    scatter_sum(1, p1, hsrc)
    last = send(hsrc, hdst, f_s.at[0], f_r.at[0], at_zh)
    p0 = scatter2(0, g0)
    scatter_sum(0, p0, fin)
    last.wait_recv()
    gin_ref[...] = (fin[...] + hdst[...]).astype(BF16)
    for cp in sent:
        cp.wait_send()


def on_device(tokens, cotangent, gate_weight, up_weight, down_weight, seq_ids, chosen, margins, counts):
    vmem = pl.BlockSpec(memory_space=pltpu.VMEM)
    smem = pl.BlockSpec(memory_space=pltpu.SMEM)
    hbm = pl.BlockSpec(memory_space=pl.ANY)
    dma = pltpu.SemaphoreType.DMA
    results = pl.pallas_call(
        kernel,
        out_shape=(
            pltpu.VMEM((ROWS, WIDTH), BF16),
            pltpu.VMEM((WIDTH, UNITS), BF16),
            pltpu.VMEM((WIDTH, UNITS), BF16),
            pltpu.VMEM((UNITS, WIDTH), BF16),
        ),
        in_specs=[hbm, hbm, hbm, hbm, hbm, smem, smem, smem, smem],
        out_specs=(vmem, vmem, vmem, vmem),
        scratch_shapes=[
            pltpu.VMEM((WIDTH, UNITS), BF16),
            pltpu.VMEM((WIDTH, UNITS), BF16),
            pltpu.VMEM((UNITS, WIDTH), BF16),
            pltpu.VMEM((2, 4, 4, ROWS, WIDTH), BF16),
            pltpu.VMEM((2, 4, 4, ROWS, WIDTH), BF16),
            pltpu.VMEM((ROWS, WIDTH), BF16),
            pltpu.VMEM((ROWS, WIDTH), BF16),
            pltpu.VMEM((3, CHUNK, UNITS), F32),
            pltpu.VMEM((2, 3, OWN, UNITS), BF16),
            pltpu.VMEM((2, 3, OWN, UNITS), BF16),
            pltpu.VMEM((2, 3, OWN, UNITS), F32),
            pltpu.VMEM((2, 3, OWN, UNITS), BF16),
            pltpu.VMEM((2, 3, OWN, UNITS), BF16),
            pltpu.VMEM((2, OWN, UNITS), F32),
            pltpu.VMEM((2, OWN, UNITS), F32),
            pltpu.VMEM((2, CHUNK, UNITS), BF16),
            pltpu.VMEM((2, 2, CHUNK, UNITS), BF16),
            pltpu.VMEM((CHUNK, WIDTH), F32),
            pltpu.VMEM((2, 4, 4, ROWS, WIDTH), BF16),
            pltpu.VMEM((2, 3, 4, ROWS, HALF), BF16),
            pltpu.VMEM((2, 3, 4, ROWS, HALF), BF16),
            pltpu.VMEM((4, ROWS, HALF), BF16),
            pltpu.VMEM((4, ROWS, HALF), BF16),
            pltpu.VMEM((2, 3, ROWS, HALF), BF16),
            pltpu.VMEM((4, ROWS, HALF), F32),
            pltpu.VMEM((4, ROWS, HALF), F32),
            pltpu.VMEM((2, 3, ROWS, HALF), F32),
            pltpu.VMEM((ROWS, WIDTH), F32),
            pltpu.VMEM((ROWS, WIDTH), F32),
            pltpu.VMEM((ROWS, WIDTH), F32),
            dma((5,)),
            dma((2,)),
            dma((2,)),
            dma((2, 2, 2, 2, 3)),
            dma((2, 2, 2, 2, 3)),
            dma((2, 3)),
            dma((2, 3)),
            dma((2, 3, 2)),
            dma((2, 3, 2)),
            dma((2,)),
            dma((2,)),
            dma((2, 2)),
            dma((2, 2)),
            dma((2, 2, 2, 3)),
            dma((2, 2, 2, 3)),
            dma((1,)),
            dma((1,)),
        ],
        compiler_params=pltpu.CompilerParams(
            collective_id=0, has_side_effects=True, vmem_limit_bytes=46 << 20
        ),
        cost_estimate=pl.CostEstimate(flops=15_000_000_000, bytes_accessed=22_000_000, transcendentals=0),
        name="simpo_backward",
    )(tokens, cotangent, gate_weight, up_weight, down_weight, seq_ids, chosen, margins, counts)
    return write_out(*results)


def write_out(*grads):
    count = len(grads)

    def body(*refs):
        sem = refs[-1]
        copies = [pltpu.make_async_copy(refs[i], refs[count + i], sem.at[i]) for i in range(count)]
        for cp in copies:
            cp.start()
        for cp in copies:
            cp.wait()

    return pl.pallas_call(
        body,
        out_shape=tuple(jax.ShapeDtypeStruct(g.shape, g.dtype) for g in grads),
        in_specs=[pl.BlockSpec(memory_space=pltpu.VMEM)] * count,
        out_specs=(pl.BlockSpec(memory_space=pl.ANY),) * count,
        scratch_shapes=[pltpu.SemaphoreType.DMA((count,))],
        compiler_params=pltpu.CompilerParams(vmem_limit_bytes=1 << 20),
        name="write_out",
    )(*grads)


def solution(mesh):
    return jax.shard_map(
        on_device,
        mesh=mesh,
        in_specs=(
            P(("out", "dep"), "inp"),
            P(("out", "dep"), "inp"),
            P("inp", ("out", "dep")),
            P("inp", ("out", "dep")),
            P(("out", "dep"), "inp"),
            P(("out", "dep")),
            P(("out", "dep")),
            P(),
            P(),
        ),
        out_specs=(
            P(("out", "dep"), "inp"),
            P("inp", ("out", "dep")),
            P("inp", ("out", "dep")),
            P(("out", "dep"), "inp"),
        ),
        check_vma=False,
    )
```

```python
import jax
import jax.numpy as jnp
from jax import lax
from jax.experimental import pallas as pl
from jax.experimental.pallas import tpu as pltpu
from jax.sharding import PartitionSpec as P

SIMPO_BETA = 2.5
LOSS_SCALE = 64.0
MESH = pl.DeviceIdType.MESH
BF16 = jnp.bfloat16
F32 = jnp.float32

WIDTH = 2048
HALF = 1024
UNITS = 896
ROWS = 16
TOKENS = 512
CHUNKS = ((0, 0), (128, 64), (256, 128), (384, 192))
ROWS_C = 128
SHARE = 64


def dot(left, right, dims):
    return lax.dot_general(left, right, (dims, ((), ())), preferred_element_type=F32)


def kernel(
    tok_ref,
    cot_ref,
    gate_ref,
    up_ref,
    down_ref,
    seq_ref,
    chosen_ref,
    margin_ref,
    count_ref,
    gin_ref,
    ggate_ref,
    gup_ref,
    gdown_ref,
    wgate,
    wup,
    wdn,
    tok,
    og,
    cot,
    ogown,
    part,
    xs,
    xr,
    summed,
    zs,
    zr,
    slope,
    swished,
    hid,
    gug,
    gpart,
    ra1,
    rb1,
    sa,
    sb,
    r2,
    sa1,
    sb1,
    r21,
    fin,
    hsrc,
    hdst,
    lsem,
    hsem_s,
    hsem_r,
    ag_s,
    ag_r,
    x_s,
    x_r,
    z_s,
    z_r,
    c_s,
    c_r,
    k_s,
    k_r,
    rs_s,
    rs_r,
    f_s,
    f_r,
):
    inp, x, dep = lax.axis_index("inp"), lax.axis_index("out"), lax.axis_index("dep")
    zl, core = inp // 2, inp % 2
    y, zh = dep // 2, dep % 2
    at_x = lambda d: (inp, (x + d) % 4, dep)
    at_y = lambda d: (inp, x, ((y + d) % 4) * 2 + zh)
    at_zh = (inp, x, y * 2 + 1 - zh)
    at_core = (zl * 2 + 1 - core, x, dep)
    at_zl = ((1 - zl) * 2 + core, x, dep)

    barrier = pltpu.get_barrier_semaphore()
    greeted = [at_x(1), at_x(2), at_x(3), at_y(1), at_y(2), at_y(3), at_zh, at_core, at_zl]
    for who in greeted:
        pl.semaphore_signal(barrier, inc=1, device_id=who, device_id_type=MESH)

    def load(src, dst, i):
        cp = pltpu.make_async_copy(src, dst, lsem.at[i])
        cp.start()
        return cp

    cot_load = load(cot_ref, cot, 0)
    tok_load = load(tok_ref, tok.at[0, (x + y) % 2, x // 2, x % 2, y // 2], 1)
    gate_load = load(gate_ref, wgate, 2)
    up_load = load(up_ref, wup, 3)
    down_load = load(down_ref, wdn, 4)

    sent = []

    def send(src, dst, s_sem, r_sem, who):
        cp = pltpu.make_async_remote_copy(
            src_ref=src, dst_ref=dst, send_sem=s_sem, recv_sem=r_sem, device_id=who, device_id_type=MESH
        )
        cp.start()
        sent.append(cp)
        return cp

    def arrived(cps):
        for cp in cps:
            cp.wait_recv()

    bufs = (tok, og)
    cols_of = (pl.ds(0, HALF), pl.ds(HALF, HALF))

    def block(ref, s, x, y):
        return ref.at[s, (x + y) % 2, x // 2, x % 2, y // 2]

    def of_x(ref, s, p, x, h):
        return ref.at[s, p, x // 2, x % 2, :, :, cols_of[h]]

    def of_y(ref, s, p, y, h):
        return ref.at[s, p, :, (y + p) % 2, y // 2, :, cols_of[h]]

    def ag1(a, s, own=None):
        got = []
        mine = block(bufs[a], s, x, y)
        for d in range(1, 4):
            for h in range(2):
                spot = mine.at[:, cols_of[h]]
                src = spot if own is None else own.at[:, cols_of[h]]
                who = at_y(d) if h == 0 else at_x(d)
                got.append(send(src, spot, ag_s.at[a, s, h, 0, d - 1], ag_r.at[a, s, h, 0, d - 1], who))
        return got

    def ag2(a, s, p):
        got = []
        for d in range(1, 4):
            for h in range(2):
                spot, who = (of_x(bufs[a], s, p, x, h), at_x(d)) if h == 0 else (of_y(bufs[a], s, p, y, h), at_y(d))
                got.append(send(spot, spot, ag_s.at[a, s, h, 1 + p, d - 1], ag_r.at[a, s, h, 1 + p, d - 1], who))
        return got

    pl.semaphore_wait(barrier, len(greeted))
    t01 = ag1(0, 0, tok_ref)
    tok_hop = send(tok_ref, block(tok, 1, x, y), hsem_s.at[0], hsem_r.at[0], at_zh)

    row = lax.broadcasted_iota(jnp.int32, (ROWS, 128), 0)
    margin = jnp.zeros((ROWS, 128), F32)
    length = jnp.ones((ROWS, 128), F32)
    polarity = jnp.zeros((ROWS, 128), F32)
    for t in range(ROWS):
        pair, pick = seq_ref[t], chosen_ref[t]
        margin = jnp.where(row == t, margin_ref[pair], margin)
        length = jnp.where(row == t, count_ref[2 * pair + pick].astype(F32), length)
        polarity = jnp.where(row == t, 1.0 - 2.0 * pick.astype(F32), polarity)
    weight = polarity * SIMPO_BETA * LOSS_SCALE * jax.nn.sigmoid(-margin) / length
    cot_load.wait()
    for j in range(WIDTH // 128):
        cols = pl.ds(j * 128, 128)
        value = (cot[:, cols].astype(F32) * weight).astype(BF16)
        ogown[:, cols] = value
        og[0, (x + y) % 2, x // 2, x % 2, y // 2, :, cols] = value
    og_hop = send(ogown, block(og, 1, x, y), hsem_s.at[1], hsem_r.at[1], at_zh)

    tok_load.wait()
    arrived(t01)
    t0a = ag2(0, 0, 0)
    arrived([tok_hop])
    t1p = ag1(0, 1)

    def tokens_of(ref, cs):
        if len(cs) == 2:
            return ref[cs[0] // 2].reshape(2 * ROWS_C, WIDTH)
        return ref[cs[0] // 2, cs[0] % 2].reshape(ROWS_C, WIDTH)

    xcp = {}
    zcp = {}

    def multiply(p, *cs):
        if p == 0:
            value = dot(tokens_of(tok, cs), wgate[...], ((1,), (0,)))
        elif p == 1:
            value = dot(tokens_of(tok, cs), wup[...], ((1,), (0,)))
        else:
            value = dot(tokens_of(og, cs), wdn[...], ((1,), (1,)))
        part[p, pl.ds(CHUNKS[cs[0]][0], len(cs) * ROWS_C)] = value
        for c in cs:
            row0, first = CHUNKS[c]
            share = pl.ds(first, SHARE)
            xs[p, share] = part[p, pl.ds(pl.multiple_of(row0 + (1 - core) * SHARE, SHARE), SHARE)].astype(BF16)
            xcp[c, p] = send(xs.at[p, share], xr.at[p, share], x_s.at[c, p], x_r.at[c, p], at_core)

    def pair_sum(p, *cs):
        for c in cs:
            xcp[c, p].wait_recv()
            row0, first = CHUNKS[c]
            share = pl.ds(first, SHARE)
            total = part[p, pl.ds(pl.multiple_of(row0 + core * SHARE, SHARE), SHARE)] + xr[p, share].astype(F32)
            summed[p, share] = total
            zs[p, share] = total.astype(BF16)
            zcp[c, p] = send(zs.at[p, share], zr.at[p, share], z_s.at[c, p], z_r.at[c, p], at_zl)

    def by_rows(c, body):
        row0, first = CHUNKS[c]

        def step(i, carry):
            body(
                pl.ds(pl.multiple_of(first + i * 16, 16), 16),
                pl.ds(pl.multiple_of(row0 + core * SHARE + i * 16, 16), 16),
            )
            return carry

        lax.fori_loop(0, SHARE // 16, step, 0)
        return pl.ds(pl.multiple_of(row0 + core * SHARE, SHARE), SHARE)

    def activate(c):
        zcp[c, 0].wait_recv()
        zcp[c, 1].wait_recv()

        def body(rows, at):
            gate_sum = summed[0, rows] + zr[0, rows].astype(F32)
            up_sum = summed[1, rows] + zr[1, rows].astype(F32)
            logistic = jax.nn.sigmoid(gate_sum)
            swish = gate_sum * logistic
            slope[rows] = up_sum * logistic * (1.0 + gate_sum * (1.0 - logistic))
            swished[rows] = swish
            hid[at] = (swish * up_sum).astype(BF16)

        spot = hid.at[by_rows(c, body)]
        return send(spot, spot, c_s.at[c], c_r.at[c], at_core)

    def act_grad(c):
        zcp[c, 2].wait_recv()

        def body(rows, at):
            hg = summed[2, rows] + zr[2, rows].astype(F32)
            gug[0, at] = (hg * slope[rows]).astype(BF16)
            gug[1, at] = (hg * swished[rows]).astype(BF16)

        spot = gug.at[:, by_rows(c, body)]
        return send(spot, spot, k_s.at[c], k_r.at[c], at_core)

    def grad_in(cs, cps, between=None):
        arrived(cps)
        span = pl.ds(CHUNKS[cs[0]][0], len(cs) * ROWS_C)
        planes = [(c // 2, c % 2) for c in cs]
        got = []
        for h in range(2):
            for q in range(2):
                wide = pl.ds(h * HALF + q * 512, 512)
                value = dot(gug[0, span], wgate[wide, :], ((1,), (1,)))
                value += dot(gug[1, span], wup[wide, :], ((1,), (1,)))
                value = value.astype(BF16).reshape(len(planes), 2, 2, 2, ROWS, 512)
                for i, (s, p) in enumerate(planes):
                    gpart[s, p, :, :, :, :, wide] = value[i]
            for d in range(1, 4):
                for s, p in planes:
                    if h == 0:
                        src, dst, who = of_x(gpart, s, p, (x + d) % 4, 0), ra1.at[s, p, d - 1], at_x(d)
                    else:
                        src, dst, who = of_y(gpart, s, p, (y + d) % 4, 1), rb1.at[s, p, d - 1], at_y(d)
                    got.append(send(src, dst, rs_s.at[s, h, p, d - 1], rs_r.at[s, h, p, d - 1], who))
            if h == 0 and between is not None:
                between()
        return got

    def first_sum(s, p, cps):
        arrived(cps)
        at_a, at_b = ((sa, sb), (sa1, sb1))[s]
        total = gpart[s, p, x // 2, x % 2, :, :, cols_of[0]].astype(F32)
        for d in range(3):
            total += ra1[s, p, d].astype(F32)
        at_a[p] = total.astype(at_a.dtype)
        total = gpart[s, p, :, (y + p) % 2, y // 2, :, cols_of[1]].astype(F32)
        for d in range(3):
            total += rb1[s, p, d].astype(F32)
        at_b[p] = total.astype(at_b.dtype)

    def pick_a(ref, y):
        return ref.at[(x + y) % 2, y // 2]

    def pick_b(ref, x):
        return ref.at[(x + y) % 2, x // 2]

    def scatter2(s):
        at_a, at_b, to = ((sa, sb, r2), (sa1, sb1, r21))[s]
        got = []
        for d in range(1, 4):
            sides = (
                (pick_a(at_a, (y + d) % 4), at_y(d)),
                (pick_b(at_b, (x + d) % 4), at_x(d)),
            )
            for h, (src, who) in enumerate(sides):
                got.append(send(src, to.at[h, d - 1], rs_s.at[s, h, 2, d - 1], rs_r.at[s, h, 2, d - 1], who))
        return got

    def scatter_sum(s, cps, out):
        arrived(cps)
        at_a, at_b, to = ((sa, sb, r2), (sa1, sb1, r21))[s]
        for h, own in enumerate((pick_a(at_a, y), pick_b(at_b, x))):
            total = own[...].astype(F32)
            for d in range(3):
                total += to[h, d].astype(F32)
            out[:, cols_of[h]] = total

    gate_load.wait()
    up_load.wait()
    arrived(t0a)
    arrived(t1p)
    t1a = ag2(0, 1, 0)
    multiply(0, 0)
    multiply(1, 0)
    t1b = ag2(0, 1, 1)
    pair_sum(0, 0)
    pair_sum(1, 0)
    arrived([og_hop])
    o1p = ag1(1, 1)
    arrived(t1a)
    multiply(0, 2)
    arrived(o1p)
    o1a = ag2(1, 1, 0)
    multiply(1, 2)
    o0p = ag1(1, 0, ogown)
    pair_sum(0, 2)
    pair_sum(1, 2)
    o1b = ag2(1, 1, 1)
    arrived(t1b)
    multiply(0, 3)
    multiply(1, 3)
    arrived(o0p)
    o0a = ag2(1, 0, 0)
    pair_sum(0, 3)
    pair_sum(1, 3)
    t0b = ag2(0, 0, 1)
    down_load.wait()
    arrived(o1a)
    multiply(2, 2)
    o0b = ag2(1, 0, 1)
    hid0 = activate(0)
    pair_sum(2, 2)
    arrived(o1b)
    multiply(2, 3)
    hid2 = activate(2)
    pair_sum(2, 3)
    arrived(o0a)
    multiply(2, 0)
    arrived(t0b)
    multiply(0, 1)
    pair_sum(2, 0)
    multiply(1, 1)
    pair_sum(0, 1)
    pair_sum(1, 1)
    hid3 = activate(3)
    k2 = act_grad(2)
    k3 = act_grad(3)
    arrived(o0b)
    multiply(2, 1)
    pair_sum(2, 1)
    later = []
    g23 = grad_in((2, 3), (k2, k3), lambda: later.append(act_grad(0)))
    g0 = grad_in((0,), later, lambda: later.append(activate(1)))
    k1 = act_grad(1)
    arrived([hid0, later[1], hid2, hid3])

    def down_tile(i, carry):
        rows = pl.ds(pl.multiple_of(i * 128, 128), 128)
        value = dot(hid[:, rows], og[...].reshape(TOKENS, WIDTH), ((0,), (0,)))
        gdown_ref[rows, :] = value.astype(BF16)
        return carry

    lax.fori_loop(0, 4, down_tile, 0)
    p1 = []

    def between():
        first_sum(1, 0, g23[0::2])
        first_sum(1, 1, g23[1::2])
        p1.extend(scatter2(1))

    g1 = grad_in((1,), (k1,), between)

    def gate_tile(i, carry):
        rows = pl.ds(pl.multiple_of(i * 256, 256), 256)
        left = tok[:, :, :, :, :, :, rows].reshape(TOKENS, 256)
        value = dot(left, jnp.concatenate([gug[0], gug[1]], axis=1), ((0,), (0,)))
        ggate_ref[rows, :] = value[:, :UNITS].astype(BF16)
        gup_ref[rows, :] = value[:, UNITS:].astype(BF16)
        return carry

    first_sum(0, 0, g0)
    lax.fori_loop(0, 5, gate_tile, 0)
    first_sum(0, 1, g1)
    p0 = scatter2(0)
    scatter_sum(1, p1, hsrc)
    last = send(hsrc, hdst, f_s.at[0], f_r.at[0], at_zh)
    lax.fori_loop(5, 8, gate_tile, 0)
    lax.fori_loop(4, UNITS // 128, down_tile, 0)
    scatter_sum(0, p0, fin)
    last.wait_recv()
    gin_ref[...] = (fin[...] + hdst[...]).astype(BF16)
    for cp in sent:
        cp.wait_send()


def on_device(tokens, cotangent, gate_weight, up_weight, down_weight, seq_ids, chosen, margins, counts):
    vmem = pl.BlockSpec(memory_space=pltpu.VMEM)
    smem = pl.BlockSpec(memory_space=pltpu.SMEM)
    hbm = pl.BlockSpec(memory_space=pl.ANY)
    dma = pltpu.SemaphoreType.DMA
    results = pl.pallas_call(
        kernel,
        out_shape=(
            pltpu.VMEM((ROWS, WIDTH), BF16),
            pltpu.VMEM((WIDTH, UNITS), BF16),
            pltpu.VMEM((WIDTH, UNITS), BF16),
            pltpu.VMEM((UNITS, WIDTH), BF16),
        ),
        in_specs=[hbm, hbm, hbm, hbm, hbm, smem, smem, smem, smem],
        out_specs=(vmem, vmem, vmem, vmem),
        scratch_shapes=[
            pltpu.VMEM((WIDTH, UNITS), BF16),
            pltpu.VMEM((WIDTH, UNITS), BF16),
            pltpu.VMEM((UNITS, WIDTH), BF16),
            pltpu.VMEM((2, 2, 2, 2, 2, ROWS, WIDTH), BF16),
            pltpu.VMEM((2, 2, 2, 2, 2, ROWS, WIDTH), BF16),
            pltpu.VMEM((ROWS, WIDTH), BF16),
            pltpu.VMEM((ROWS, WIDTH), BF16),
            pltpu.VMEM((3, TOKENS, UNITS), F32),
            pltpu.VMEM((3, 256, UNITS), BF16),
            pltpu.VMEM((3, 256, UNITS), BF16),
            pltpu.VMEM((3, 256, UNITS), F32),
            pltpu.VMEM((3, 256, UNITS), BF16),
            pltpu.VMEM((3, 256, UNITS), BF16),
            pltpu.VMEM((256, UNITS), F32),
            pltpu.VMEM((256, UNITS), F32),
            pltpu.VMEM((TOKENS, UNITS), BF16),
            pltpu.VMEM((2, TOKENS, UNITS), BF16),
            pltpu.VMEM((2, 2, 2, 2, 2, ROWS, WIDTH), BF16),
            pltpu.VMEM((2, 2, 3, 2, ROWS, HALF), BF16),
            pltpu.VMEM((2, 2, 3, 2, ROWS, HALF), BF16),
            pltpu.VMEM((2, 2, ROWS, HALF), BF16),
            pltpu.VMEM((2, 2, ROWS, HALF), BF16),
            pltpu.VMEM((2, 3, ROWS, HALF), BF16),
            pltpu.VMEM((2, 2, ROWS, HALF), BF16),
            pltpu.VMEM((2, 2, ROWS, HALF), BF16),
            pltpu.VMEM((2, 3, ROWS, HALF), BF16),
            pltpu.VMEM((ROWS, WIDTH), F32),
            pltpu.VMEM((ROWS, WIDTH), F32),
            pltpu.VMEM((ROWS, WIDTH), F32),
            dma((5,)),
            dma((2,)),
            dma((2,)),
            dma((2, 2, 2, 3, 3)),
            dma((2, 2, 2, 3, 3)),
            dma((4, 3)),
            dma((4, 3)),
            dma((4, 3)),
            dma((4, 3)),
            dma((4,)),
            dma((4,)),
            dma((4,)),
            dma((4,)),
            dma((2, 2, 3, 3)),
            dma((2, 2, 3, 3)),
            dma((1,)),
            dma((1,)),
        ],
        compiler_params=pltpu.CompilerParams(
            collective_id=0, has_side_effects=True, vmem_limit_bytes=46 << 20
        ),
        cost_estimate=pl.CostEstimate(flops=15_000_000_000, bytes_accessed=22_000_000, transcendentals=0),
        name="simpo_backward",
    )(tokens, cotangent, gate_weight, up_weight, down_weight, seq_ids, chosen, margins, counts)
    return write_out(*results)


def write_out(*grads):
    count = len(grads)

    def body(*refs):
        sem = refs[-1]
        copies = [pltpu.make_async_copy(refs[i], refs[count + i], sem.at[i]) for i in range(count)]
        for cp in copies:
            cp.start()
        for cp in copies:
            cp.wait()

    return pl.pallas_call(
        body,
        out_shape=tuple(jax.ShapeDtypeStruct(g.shape, g.dtype) for g in grads),
        in_specs=[pl.BlockSpec(memory_space=pltpu.VMEM)] * count,
        out_specs=(pl.BlockSpec(memory_space=pl.ANY),) * count,
        scratch_shapes=[pltpu.SemaphoreType.DMA((count,))],
        compiler_params=pltpu.CompilerParams(vmem_limit_bytes=1 << 20),
        name="write_out",
    )(*grads)


def solution(mesh):
    return jax.shard_map(
        on_device,
        mesh=mesh,
        in_specs=(
            P(("out", "dep"), "inp"),
            P(("out", "dep"), "inp"),
            P("inp", ("out", "dep")),
            P("inp", ("out", "dep")),
            P(("out", "dep"), "inp"),
            P(("out", "dep")),
            P(("out", "dep")),
            P(),
            P(),
        ),
        out_specs=(
            P(("out", "dep"), "inp"),
            P("inp", ("out", "dep")),
            P("inp", ("out", "dep")),
            P(("out", "dep"), "inp"),
        ),
        check_vma=False,
    )
```

```python
import jax
import jax.numpy as jnp
from jax import lax
from jax.experimental import pallas as pl
from jax.experimental.pallas import tpu as pltpu
from jax.sharding import PartitionSpec as P

SIMPO_BETA = 2.5
LOSS_SCALE = 64.0
MESH = pl.DeviceIdType.MESH
BF16 = jnp.bfloat16
F32 = jnp.float32

WIDTH = 2048
HALF = 1024
UNITS = 896
ROWS = 16
TOKENS = 512
CHUNKS = ((0, 0), (128, 64), (256, 128), (384, 192))
ROWS_C = 128
SHARE = 64


def dot(left, right, dims):
    return lax.dot_general(left, right, (dims, ((), ())), preferred_element_type=F32)


def kernel(
    tok_ref,
    cot_ref,
    gate_ref,
    up_ref,
    down_ref,
    seq_ref,
    chosen_ref,
    margin_ref,
    count_ref,
    gin_ref,
    ggate_ref,
    gup_ref,
    gdown_ref,
    wgate,
    wup,
    wdn,
    tok,
    og,
    cot,
    ogown,
    part,
    xs,
    xr,
    summed,
    zs,
    zr,
    slope,
    swished,
    hid,
    gug,
    gpart,
    ra1,
    rb1,
    sa,
    sb,
    r2,
    sa1,
    sb1,
    r21,
    fin,
    hsrc,
    hdst,
    lsem,
    hsem_s,
    hsem_r,
    ag_s,
    ag_r,
    x_s,
    x_r,
    z_s,
    z_r,
    c_s,
    c_r,
    k_s,
    k_r,
    rs_s,
    rs_r,
    f_s,
    f_r,
):
    inp, x, dep = lax.axis_index("inp"), lax.axis_index("out"), lax.axis_index("dep")
    zl, core = inp // 2, inp % 2
    y, zh = dep // 2, dep % 2
    at_x = lambda d: (inp, (x + d) % 4, dep)
    at_y = lambda d: (inp, x, ((y + d) % 4) * 2 + zh)
    at_zh = (inp, x, y * 2 + 1 - zh)
    at_core = (zl * 2 + 1 - core, x, dep)
    at_zl = ((1 - zl) * 2 + core, x, dep)

    barrier = pltpu.get_barrier_semaphore()
    greeted = [at_x(1), at_x(2), at_x(3), at_y(1), at_y(2), at_y(3), at_zh, at_core, at_zl]
    for who in greeted:
        pl.semaphore_signal(barrier, inc=1, device_id=who, device_id_type=MESH)

    def load(src, dst, i):
        cp = pltpu.make_async_copy(src, dst, lsem.at[i])
        cp.start()
        return cp

    cot_load = load(cot_ref, cot, 0)
    tok_load = load(tok_ref, tok.at[0, (x + y) % 2, x // 2, x % 2, y // 2], 1)
    gate_load = load(gate_ref, wgate, 2)
    up_load = load(up_ref, wup, 3)
    down_load = load(down_ref, wdn, 4)

    sent = []

    def send(src, dst, s_sem, r_sem, who):
        cp = pltpu.make_async_remote_copy(
            src_ref=src, dst_ref=dst, send_sem=s_sem, recv_sem=r_sem, device_id=who, device_id_type=MESH
        )
        cp.start()
        sent.append(cp)
        return cp

    def arrived(cps):
        for cp in cps:
            cp.wait_recv()

    bufs = (tok, og)
    cols_of = (pl.ds(0, HALF), pl.ds(HALF, HALF))

    def block(ref, s, x, y):
        return ref.at[s, (x + y) % 2, x // 2, x % 2, y // 2]

    def of_x(ref, s, p, x, h):
        return ref.at[s, p, x // 2, x % 2, :, :, cols_of[h]]

    def of_y(ref, s, p, y, h):
        return ref.at[s, p, :, (y + p) % 2, y // 2, :, cols_of[h]]

    def ag1(a, s, own=None):
        got = []
        mine = block(bufs[a], s, x, y)
        for d in range(1, 4):
            for h in range(2):
                spot = mine.at[:, cols_of[h]]
                src = spot if own is None else own.at[:, cols_of[h]]
                who = at_y(d) if h == 0 else at_x(d)
                got.append(send(src, spot, ag_s.at[a, s, h, 0, d - 1], ag_r.at[a, s, h, 0, d - 1], who))
        return got

    def ag2(a, s, p):
        got = []
        for d in range(1, 4):
            for h in range(2):
                spot, who = (of_x(bufs[a], s, p, x, h), at_x(d)) if h == 0 else (of_y(bufs[a], s, p, y, h), at_y(d))
                got.append(send(spot, spot, ag_s.at[a, s, h, 1 + p, d - 1], ag_r.at[a, s, h, 1 + p, d - 1], who))
        return got

    pl.semaphore_wait(barrier, len(greeted))
    t01 = ag1(0, 0, tok_ref)
    tok_hop = send(tok_ref, block(tok, 1, x, y), hsem_s.at[0], hsem_r.at[0], at_zh)

    row = lax.broadcasted_iota(jnp.int32, (ROWS, 128), 0)
    margin = jnp.zeros((ROWS, 128), F32)
    length = jnp.ones((ROWS, 128), F32)
    polarity = jnp.zeros((ROWS, 128), F32)
    for t in range(ROWS):
        pair, pick = seq_ref[t], chosen_ref[t]
        margin = jnp.where(row == t, margin_ref[pair], margin)
        length = jnp.where(row == t, count_ref[2 * pair + pick].astype(F32), length)
        polarity = jnp.where(row == t, 1.0 - 2.0 * pick.astype(F32), polarity)
    weight = polarity * SIMPO_BETA * LOSS_SCALE * jax.nn.sigmoid(-margin) / length
    cot_load.wait()
    for j in range(WIDTH // 128):
        cols = pl.ds(j * 128, 128)
        value = (cot[:, cols].astype(F32) * weight).astype(BF16)
        ogown[:, cols] = value
        og[0, (x + y) % 2, x // 2, x % 2, y // 2, :, cols] = value
    og_hop = send(ogown, block(og, 1, x, y), hsem_s.at[1], hsem_r.at[1], at_zh)

    tok_load.wait()
    arrived(t01)
    t0a = ag2(0, 0, 0)
    arrived([tok_hop])
    t1p = ag1(0, 1)

    def tokens_of(ref, cs):
        if len(cs) == 2:
            return ref[cs[0] // 2].reshape(2 * ROWS_C, WIDTH)
        return ref[cs[0] // 2, cs[0] % 2].reshape(ROWS_C, WIDTH)

    xcp = {}
    zcp = {}

    def multiply(p, *cs):
        if p == 0:
            value = dot(tokens_of(tok, cs), wgate[...], ((1,), (0,)))
        elif p == 1:
            value = dot(tokens_of(tok, cs), wup[...], ((1,), (0,)))
        else:
            value = dot(tokens_of(og, cs), wdn[...], ((1,), (1,)))
        part[p, pl.ds(CHUNKS[cs[0]][0], len(cs) * ROWS_C)] = value
        for c in cs:
            row0, first = CHUNKS[c]
            share = pl.ds(first, SHARE)
            xs[p, share] = part[p, pl.ds(pl.multiple_of(row0 + (1 - core) * SHARE, SHARE), SHARE)].astype(BF16)
            xcp[c, p] = send(xs.at[p, share], xr.at[p, share], x_s.at[c, p], x_r.at[c, p], at_core)

    def pair_sum(p, *cs):
        for c in cs:
            xcp[c, p].wait_recv()
            row0, first = CHUNKS[c]
            share = pl.ds(first, SHARE)
            total = part[p, pl.ds(pl.multiple_of(row0 + core * SHARE, SHARE), SHARE)] + xr[p, share].astype(F32)
            summed[p, share] = total
            zs[p, share] = total.astype(BF16)
            zcp[c, p] = send(zs.at[p, share], zr.at[p, share], z_s.at[c, p], z_r.at[c, p], at_zl)

    def by_rows(c, body):
        row0, first = CHUNKS[c]

        def step(i, carry):
            body(
                pl.ds(pl.multiple_of(first + i * 16, 16), 16),
                pl.ds(pl.multiple_of(row0 + core * SHARE + i * 16, 16), 16),
            )
            return carry

        lax.fori_loop(0, SHARE // 16, step, 0)
        return pl.ds(pl.multiple_of(row0 + core * SHARE, SHARE), SHARE)

    def activate(c):
        zcp[c, 0].wait_recv()
        zcp[c, 1].wait_recv()

        def body(rows, at):
            gate_sum = summed[0, rows] + zr[0, rows].astype(F32)
            up_sum = summed[1, rows] + zr[1, rows].astype(F32)
            logistic = jax.nn.sigmoid(gate_sum)
            swish = gate_sum * logistic
            slope[rows] = up_sum * logistic * (1.0 + gate_sum * (1.0 - logistic))
            swished[rows] = swish
            hid[at] = (swish * up_sum).astype(BF16)

        spot = hid.at[by_rows(c, body)]
        return send(spot, spot, c_s.at[c], c_r.at[c], at_core)

    def act_grad(c):
        zcp[c, 2].wait_recv()

        def body(rows, at):
            hg = summed[2, rows] + zr[2, rows].astype(F32)
            gug[0, at] = (hg * slope[rows]).astype(BF16)
            gug[1, at] = (hg * swished[rows]).astype(BF16)

        spot = gug.at[:, by_rows(c, body)]
        return send(spot, spot, k_s.at[c], k_r.at[c], at_core)

    def grad_in(cs, cps, between=None):
        arrived(cps)
        span = pl.ds(CHUNKS[cs[0]][0], len(cs) * ROWS_C)
        planes = [(c // 2, c % 2) for c in cs]
        got = []
        for h in range(2):
            for q in range(2):
                wide = pl.ds(h * HALF + q * 512, 512)
                value = dot(gug[0, span], wgate[wide, :], ((1,), (1,)))
                value += dot(gug[1, span], wup[wide, :], ((1,), (1,)))
                value = value.astype(BF16).reshape(len(planes), 2, 2, 2, ROWS, 512)
                for i, (s, p) in enumerate(planes):
                    gpart[s, p, :, :, :, :, wide] = value[i]
            for d in range(1, 4):
                for s, p in planes:
                    if h == 0:
                        src, dst, who = of_x(gpart, s, p, (x + d) % 4, 0), ra1.at[s, p, d - 1], at_x(d)
                    else:
                        src, dst, who = of_y(gpart, s, p, (y + d) % 4, 1), rb1.at[s, p, d - 1], at_y(d)
                    got.append(send(src, dst, rs_s.at[s, h, p, d - 1], rs_r.at[s, h, p, d - 1], who))
            if h == 0 and between is not None:
                between()
        return got

    def first_sum(s, p, cps):
        arrived(cps)
        at_a, at_b = ((sa, sb), (sa1, sb1))[s]
        total = gpart[s, p, x // 2, x % 2, :, :, cols_of[0]].astype(F32)
        for d in range(3):
            total += ra1[s, p, d].astype(F32)
        at_a[p] = total.astype(at_a.dtype)
        total = gpart[s, p, :, (y + p) % 2, y // 2, :, cols_of[1]].astype(F32)
        for d in range(3):
            total += rb1[s, p, d].astype(F32)
        at_b[p] = total.astype(at_b.dtype)

    def pick_a(ref, y):
        return ref.at[(x + y) % 2, y // 2]

    def pick_b(ref, x):
        return ref.at[(x + y) % 2, x // 2]

    def scatter2(s):
        at_a, at_b, to = ((sa, sb, r2), (sa1, sb1, r21))[s]
        got = []
        for d in range(1, 4):
            sides = (
                (pick_a(at_a, (y + d) % 4), at_y(d)),
                (pick_b(at_b, (x + d) % 4), at_x(d)),
            )
            for h, (src, who) in enumerate(sides):
                got.append(send(src, to.at[h, d - 1], rs_s.at[s, h, 2, d - 1], rs_r.at[s, h, 2, d - 1], who))
        return got

    def scatter_sum(s, cps, out):
        arrived(cps)
        at_a, at_b, to = ((sa, sb, r2), (sa1, sb1, r21))[s]
        for h, own in enumerate((pick_a(at_a, y), pick_b(at_b, x))):
            total = own[...].astype(F32)
            for d in range(3):
                total += to[h, d].astype(F32)
            out[:, cols_of[h]] = total

    gate_load.wait()
    up_load.wait()
    arrived(t0a)
    arrived(t1p)
    t1a = ag2(0, 1, 0)
    multiply(0, 0)
    multiply(1, 0)
    pair_sum(0, 0)
    pair_sum(1, 0)
    t1b = ag2(0, 1, 1)
    arrived([og_hop])
    o1p = ag1(1, 1)
    arrived(t1a)
    multiply(0, 2)
    arrived(o1p)
    o1a = ag2(1, 1, 0)
    multiply(1, 2)
    o0p = ag1(1, 0, ogown)
    pair_sum(0, 2)
    pair_sum(1, 2)
    o1b = ag2(1, 1, 1)
    arrived(t1b)
    multiply(0, 3)
    multiply(1, 3)
    arrived(o0p)
    o0a = ag2(1, 0, 0)
    pair_sum(0, 3)
    pair_sum(1, 3)
    t0b = ag2(0, 0, 1)
    down_load.wait()
    arrived(o1a)
    multiply(2, 2)
    o0b = ag2(1, 0, 1)
    hid0 = activate(0)
    pair_sum(2, 2)
    arrived(o1b)
    multiply(2, 3)
    hid2 = activate(2)
    pair_sum(2, 3)
    arrived(o0a)
    multiply(2, 0)
    arrived(t0b)
    multiply(0, 1)
    pair_sum(2, 0)
    multiply(1, 1)
    pair_sum(0, 1)
    pair_sum(1, 1)
    hid3 = activate(3)
    k2 = act_grad(2)
    k3 = act_grad(3)
    arrived(o0b)
    multiply(2, 1)
    pair_sum(2, 1)
    later = []
    g23 = grad_in((2, 3), (k2, k3), lambda: later.append(act_grad(0)))
    g0 = grad_in((0,), later, lambda: later.append(activate(1)))
    k1 = act_grad(1)
    arrived([hid0, later[1], hid2, hid3])

    def down_tile(i, carry):
        rows = pl.ds(pl.multiple_of(i * 128, 128), 128)
        value = dot(hid[:, rows], og[...].reshape(TOKENS, WIDTH), ((0,), (0,)))
        gdown_ref[rows, :] = value.astype(BF16)
        return carry

    lax.fori_loop(0, 4, down_tile, 0)
    p1 = []

    def between():
        first_sum(1, 0, g23[0::2])
        first_sum(1, 1, g23[1::2])
        p1.extend(scatter2(1))

    g1 = grad_in((1,), (k1,), between)

    def gate_tile(i, carry):
        rows = pl.ds(pl.multiple_of(i * 256, 256), 256)
        left = tok[:, :, :, :, :, :, rows].reshape(TOKENS, 256)
        value = dot(left, jnp.concatenate([gug[0], gug[1]], axis=1), ((0,), (0,)))
        ggate_ref[rows, :] = value[:, :UNITS].astype(BF16)
        gup_ref[rows, :] = value[:, UNITS:].astype(BF16)
        return carry

    first_sum(0, 0, g0)
    lax.fori_loop(0, 4, gate_tile, 0)
    first_sum(0, 1, g1)
    p0 = scatter2(0)
    scatter_sum(1, p1, hsrc)
    last = send(hsrc, hdst, f_s.at[0], f_r.at[0], at_zh)
    lax.fori_loop(4, 8, gate_tile, 0)
    lax.fori_loop(4, UNITS // 128, down_tile, 0)
    scatter_sum(0, p0, fin)
    last.wait_recv()
    gin_ref[...] = (fin[...] + hdst[...]).astype(BF16)
    for cp in sent:
        cp.wait_send()


def on_device(tokens, cotangent, gate_weight, up_weight, down_weight, seq_ids, chosen, margins, counts):
    vmem = pl.BlockSpec(memory_space=pltpu.VMEM)
    smem = pl.BlockSpec(memory_space=pltpu.SMEM)
    hbm = pl.BlockSpec(memory_space=pl.ANY)
    dma = pltpu.SemaphoreType.DMA
    results = pl.pallas_call(
        kernel,
        out_shape=(
            pltpu.VMEM((ROWS, WIDTH), BF16),
            pltpu.VMEM((WIDTH, UNITS), BF16),
            pltpu.VMEM((WIDTH, UNITS), BF16),
            pltpu.VMEM((UNITS, WIDTH), BF16),
        ),
        in_specs=[hbm, hbm, hbm, hbm, hbm, smem, smem, smem, smem],
        out_specs=(vmem, vmem, vmem, vmem),
        scratch_shapes=[
            pltpu.VMEM((WIDTH, UNITS), BF16),
            pltpu.VMEM((WIDTH, UNITS), BF16),
            pltpu.VMEM((UNITS, WIDTH), BF16),
            pltpu.VMEM((2, 2, 2, 2, 2, ROWS, WIDTH), BF16),
            pltpu.VMEM((2, 2, 2, 2, 2, ROWS, WIDTH), BF16),
            pltpu.VMEM((ROWS, WIDTH), BF16),
            pltpu.VMEM((ROWS, WIDTH), BF16),
            pltpu.VMEM((3, TOKENS, UNITS), F32),
            pltpu.VMEM((3, 256, UNITS), BF16),
            pltpu.VMEM((3, 256, UNITS), BF16),
            pltpu.VMEM((3, 256, UNITS), F32),
            pltpu.VMEM((3, 256, UNITS), BF16),
            pltpu.VMEM((3, 256, UNITS), BF16),
            pltpu.VMEM((256, UNITS), F32),
            pltpu.VMEM((256, UNITS), F32),
            pltpu.VMEM((TOKENS, UNITS), BF16),
            pltpu.VMEM((2, TOKENS, UNITS), BF16),
            pltpu.VMEM((2, 2, 2, 2, 2, ROWS, WIDTH), BF16),
            pltpu.VMEM((2, 2, 3, 2, ROWS, HALF), BF16),
            pltpu.VMEM((2, 2, 3, 2, ROWS, HALF), BF16),
            pltpu.VMEM((2, 2, ROWS, HALF), BF16),
            pltpu.VMEM((2, 2, ROWS, HALF), BF16),
            pltpu.VMEM((2, 3, ROWS, HALF), BF16),
            pltpu.VMEM((2, 2, ROWS, HALF), BF16),
            pltpu.VMEM((2, 2, ROWS, HALF), BF16),
            pltpu.VMEM((2, 3, ROWS, HALF), BF16),
            pltpu.VMEM((ROWS, WIDTH), F32),
            pltpu.VMEM((ROWS, WIDTH), F32),
            pltpu.VMEM((ROWS, WIDTH), F32),
            dma((5,)),
            dma((2,)),
            dma((2,)),
            dma((2, 2, 2, 3, 3)),
            dma((2, 2, 2, 3, 3)),
            dma((4, 3)),
            dma((4, 3)),
            dma((4, 3)),
            dma((4, 3)),
            dma((4,)),
            dma((4,)),
            dma((4,)),
            dma((4,)),
            dma((2, 2, 3, 3)),
            dma((2, 2, 3, 3)),
            dma((1,)),
            dma((1,)),
        ],
        compiler_params=pltpu.CompilerParams(
            collective_id=0, has_side_effects=True, vmem_limit_bytes=46 << 20
        ),
        cost_estimate=pl.CostEstimate(flops=15_000_000_000, bytes_accessed=22_000_000, transcendentals=0),
        name="simpo_backward",
    )(tokens, cotangent, gate_weight, up_weight, down_weight, seq_ids, chosen, margins, counts)
    return write_out(*results)


def write_out(*grads):
    count = len(grads)

    def body(*refs):
        sem = refs[-1]
        copies = [pltpu.make_async_copy(refs[0], refs[count], sem.at[0, 0])]
        for i in range(1, count):
            part = grads[i].shape[0] // 4
            for j in range(4):
                rows = pl.ds(j * part, part)
                copies.append(pltpu.make_async_copy(refs[i].at[rows], refs[count + i].at[rows], sem.at[i, j]))
        for cp in copies:
            cp.start()
        for cp in copies:
            cp.wait()

    return pl.pallas_call(
        body,
        out_shape=tuple(jax.ShapeDtypeStruct(g.shape, g.dtype) for g in grads),
        in_specs=[pl.BlockSpec(memory_space=pltpu.VMEM)] * count,
        out_specs=(pl.BlockSpec(memory_space=pl.ANY),) * count,
        scratch_shapes=[pltpu.SemaphoreType.DMA((count, 4))],
        compiler_params=pltpu.CompilerParams(vmem_limit_bytes=1 << 20),
        name="write_out",
    )(*grads)


def solution(mesh):
    return jax.shard_map(
        on_device,
        mesh=mesh,
        in_specs=(
            P(("out", "dep"), "inp"),
            P(("out", "dep"), "inp"),
            P("inp", ("out", "dep")),
            P("inp", ("out", "dep")),
            P(("out", "dep"), "inp"),
            P(("out", "dep")),
            P(("out", "dep")),
            P(),
            P(),
        ),
        out_specs=(
            P(("out", "dep"), "inp"),
            P("inp", ("out", "dep")),
            P("inp", ("out", "dep")),
            P(("out", "dep"), "inp"),
        ),
        check_vma=False,
    )
```

```python
import jax
import jax.numpy as jnp
from jax import lax
from jax.experimental import pallas as pl
from jax.experimental.pallas import tpu as pltpu
from jax.sharding import PartitionSpec as P

SIMPO_BETA = 2.5
LOSS_SCALE = 64.0
MESH = pl.DeviceIdType.MESH
BF16 = jnp.bfloat16
F32 = jnp.float32

WIDTH = 2048
HALF = 1024
UNITS = 896
ROWS = 16
TOKENS = 512
CHUNKS = ((0, 0), (128, 64), (256, 128), (384, 192))
ROWS_C = 128
SHARE = 64


def dot(left, right, dims):
    return lax.dot_general(left, right, (dims, ((), ())), preferred_element_type=F32)


def kernel(
    tok_ref,
    cot_ref,
    gate_ref,
    up_ref,
    down_ref,
    seq_ref,
    chosen_ref,
    margin_ref,
    count_ref,
    gin_ref,
    ggate_ref,
    gup_ref,
    gdown_ref,
    wgate,
    wup,
    wdn,
    tok,
    og,
    cot,
    ogown,
    part,
    xs,
    xr,
    summed,
    zs,
    zr,
    slope,
    swished,
    hid,
    gug,
    gpart,
    ra1,
    rb1,
    sa,
    sb,
    r2,
    sa1,
    sb1,
    r21,
    fin,
    hsrc,
    hdst,
    lsem,
    hsem_s,
    hsem_r,
    ag_s,
    ag_r,
    x_s,
    x_r,
    z_s,
    z_r,
    c_s,
    c_r,
    k_s,
    k_r,
    rs_s,
    rs_r,
    f_s,
    f_r,
):
    inp, x, dep = lax.axis_index("inp"), lax.axis_index("out"), lax.axis_index("dep")
    zl, core = inp // 2, inp % 2
    y, zh = dep // 2, dep % 2
    at_x = lambda d: (inp, (x + d) % 4, dep)
    at_y = lambda d: (inp, x, ((y + d) % 4) * 2 + zh)
    at_zh = (inp, x, y * 2 + 1 - zh)
    at_core = (zl * 2 + 1 - core, x, dep)
    at_zl = ((1 - zl) * 2 + core, x, dep)

    barrier = pltpu.get_barrier_semaphore()
    greeted = [at_x(1), at_x(2), at_x(3), at_y(1), at_y(2), at_y(3), at_zh, at_core, at_zl]
    for who in greeted:
        pl.semaphore_signal(barrier, inc=1, device_id=who, device_id_type=MESH)

    def load(src, dst, i):
        cp = pltpu.make_async_copy(src, dst, lsem.at[i])
        cp.start()
        return cp

    cot_load = load(cot_ref, cot, 0)
    tok_load = load(tok_ref, tok.at[0, (x + y) % 2, x // 2, x % 2, y // 2], 1)
    gate_load = load(gate_ref, wgate, 2)
    up_load = load(up_ref, wup, 3)
    down_load = load(down_ref, wdn, 4)

    sent = []

    def send(src, dst, s_sem, r_sem, who):
        cp = pltpu.make_async_remote_copy(
            src_ref=src, dst_ref=dst, send_sem=s_sem, recv_sem=r_sem, device_id=who, device_id_type=MESH
        )
        cp.start()
        sent.append(cp)
        return cp

    def arrived(cps):
        for cp in cps:
            cp.wait_recv()

    bufs = (tok, og)
    cols_of = (pl.ds(0, HALF), pl.ds(HALF, HALF))

    def block(ref, s, x, y):
        return ref.at[s, (x + y) % 2, x // 2, x % 2, y // 2]

    def of_x(ref, s, p, x, h):
        return ref.at[s, p, x // 2, x % 2, :, :, cols_of[h]]

    def of_y(ref, s, p, y, h):
        return ref.at[s, p, :, (y + p) % 2, y // 2, :, cols_of[h]]

    def ag1(a, s, own=None):
        got = []
        mine = block(bufs[a], s, x, y)
        for d in range(1, 4):
            for h in range(2):
                spot = mine.at[:, cols_of[h]]
                src = spot if own is None else own.at[:, cols_of[h]]
                who = at_y(d) if h == 0 else at_x(d)
                got.append(send(src, spot, ag_s.at[a, s, h, 0, d - 1], ag_r.at[a, s, h, 0, d - 1], who))
        return got

    def ag2(a, s, p):
        got = []
        for d in range(1, 4):
            for h in range(2):
                spot, who = (of_x(bufs[a], s, p, x, h), at_x(d)) if h == 0 else (of_y(bufs[a], s, p, y, h), at_y(d))
                got.append(send(spot, spot, ag_s.at[a, s, h, 1 + p, d - 1], ag_r.at[a, s, h, 1 + p, d - 1], who))
        return got

    pl.semaphore_wait(barrier, len(greeted))
    t01 = ag1(0, 0, tok_ref)
    tok_hop = send(tok_ref, block(tok, 1, x, y), hsem_s.at[0], hsem_r.at[0], at_zh)

    row = lax.broadcasted_iota(jnp.int32, (ROWS, 128), 0)
    margin = jnp.zeros((ROWS, 128), F32)
    length = jnp.ones((ROWS, 128), F32)
    polarity = jnp.zeros((ROWS, 128), F32)
    for t in range(ROWS):
        pair, pick = seq_ref[t], chosen_ref[t]
        margin = jnp.where(row == t, margin_ref[pair], margin)
        length = jnp.where(row == t, count_ref[2 * pair + pick].astype(F32), length)
        polarity = jnp.where(row == t, 1.0 - 2.0 * pick.astype(F32), polarity)
    weight = polarity * SIMPO_BETA * LOSS_SCALE * jax.nn.sigmoid(-margin) / length
    cot_load.wait()
    for j in range(WIDTH // 128):
        cols = pl.ds(j * 128, 128)
        value = (cot[:, cols].astype(F32) * weight).astype(BF16)
        ogown[:, cols] = value
        og[0, (x + y) % 2, x // 2, x % 2, y // 2, :, cols] = value
    og_hop = send(ogown, block(og, 1, x, y), hsem_s.at[1], hsem_r.at[1], at_zh)

    tok_load.wait()
    arrived(t01)
    t0a = ag2(0, 0, 0)
    arrived([tok_hop])
    t1p = ag1(0, 1)

    def tokens_of(ref, cs):
        if len(cs) == 2:
            return ref[cs[0] // 2].reshape(2 * ROWS_C, WIDTH)
        return ref[cs[0] // 2, cs[0] % 2].reshape(ROWS_C, WIDTH)

    xcp = {}
    zcp = {}

    def multiply(p, *cs):
        if p == 0:
            value = dot(tokens_of(tok, cs), wgate[...], ((1,), (0,)))
        elif p == 1:
            value = dot(tokens_of(tok, cs), wup[...], ((1,), (0,)))
        else:
            value = dot(tokens_of(og, cs), wdn[...], ((1,), (1,)))
        part[p, pl.ds(CHUNKS[cs[0]][0], len(cs) * ROWS_C)] = value
        for c in cs:
            row0, first = CHUNKS[c]
            share = pl.ds(first, SHARE)
            xs[p, share] = part[p, pl.ds(pl.multiple_of(row0 + (1 - core) * SHARE, SHARE), SHARE)].astype(BF16)
            xcp[c, p] = send(xs.at[p, share], xr.at[p, share], x_s.at[c, p], x_r.at[c, p], at_core)

    def pair_sum(p, *cs):
        for c in cs:
            xcp[c, p].wait_recv()
            row0, first = CHUNKS[c]
            share = pl.ds(first, SHARE)
            total = part[p, pl.ds(pl.multiple_of(row0 + core * SHARE, SHARE), SHARE)] + xr[p, share].astype(F32)
            summed[p, share] = total
            zs[p, share] = total.astype(BF16)
            zcp[c, p] = send(zs.at[p, share], zr.at[p, share], z_s.at[c, p], z_r.at[c, p], at_zl)

    def by_rows(c, body):
        row0, first = CHUNKS[c]

        def step(i, carry):
            body(
                pl.ds(pl.multiple_of(first + i * 16, 16), 16),
                pl.ds(pl.multiple_of(row0 + core * SHARE + i * 16, 16), 16),
            )
            return carry

        lax.fori_loop(0, SHARE // 16, step, 0)
        return pl.ds(pl.multiple_of(row0 + core * SHARE, SHARE), SHARE)

    def activate(c):
        zcp[c, 0].wait_recv()
        zcp[c, 1].wait_recv()

        def body(rows, at):
            gate_sum = summed[0, rows] + zr[0, rows].astype(F32)
            up_sum = summed[1, rows] + zr[1, rows].astype(F32)
            logistic = jax.nn.sigmoid(gate_sum)
            swish = gate_sum * logistic
            slope[rows] = up_sum * logistic * (1.0 + gate_sum * (1.0 - logistic))
            swished[rows] = swish
            hid[at] = (swish * up_sum).astype(BF16)

        spot = hid.at[by_rows(c, body)]
        return send(spot, spot, c_s.at[c], c_r.at[c], at_core)

    def act_grad(c):
        zcp[c, 2].wait_recv()

        def body(rows, at):
            hg = summed[2, rows] + zr[2, rows].astype(F32)
            gug[0, at] = (hg * slope[rows]).astype(BF16)
            gug[1, at] = (hg * swished[rows]).astype(BF16)

        spot = gug.at[:, by_rows(c, body)]
        return send(spot, spot, k_s.at[c], k_r.at[c], at_core)

    def grad_in(cs, cps, between=None):
        arrived(cps)
        span = pl.ds(CHUNKS[cs[0]][0], len(cs) * ROWS_C)
        planes = [(c // 2, c % 2) for c in cs]
        got = []
        for h in range(2):
            for q in range(2):
                wide = pl.ds(h * HALF + q * 512, 512)
                value = dot(gug[0, span], wgate[wide, :], ((1,), (1,)))
                value += dot(gug[1, span], wup[wide, :], ((1,), (1,)))
                value = value.astype(BF16).reshape(len(planes), 2, 2, 2, ROWS, 512)
                for i, (s, p) in enumerate(planes):
                    gpart[s, p, :, :, :, :, wide] = value[i]
            for d in range(1, 4):
                for s, p in planes:
                    if h == 0:
                        src, dst, who = of_x(gpart, s, p, (x + d) % 4, 0), ra1.at[s, p, d - 1], at_x(d)
                    else:
                        src, dst, who = of_y(gpart, s, p, (y + d) % 4, 1), rb1.at[s, p, d - 1], at_y(d)
                    got.append(send(src, dst, rs_s.at[s, h, p, d - 1], rs_r.at[s, h, p, d - 1], who))
            if h == 0 and between is not None:
                between()
        return got

    def first_sum(s, p, cps):
        arrived(cps)
        at_a, at_b = ((sa, sb), (sa1, sb1))[s]
        total = gpart[s, p, x // 2, x % 2, :, :, cols_of[0]].astype(F32)
        for d in range(3):
            total += ra1[s, p, d].astype(F32)
        at_a[p] = total.astype(at_a.dtype)
        total = gpart[s, p, :, (y + p) % 2, y // 2, :, cols_of[1]].astype(F32)
        for d in range(3):
            total += rb1[s, p, d].astype(F32)
        at_b[p] = total.astype(at_b.dtype)

    def pick_a(ref, y):
        return ref.at[(x + y) % 2, y // 2]

    def pick_b(ref, x):
        return ref.at[(x + y) % 2, x // 2]

    def scatter2(s):
        at_a, at_b, to = ((sa, sb, r2), (sa1, sb1, r21))[s]
        got = []
        for d in range(1, 4):
            sides = (
                (pick_a(at_a, (y + d) % 4), at_y(d)),
                (pick_b(at_b, (x + d) % 4), at_x(d)),
            )
            for h, (src, who) in enumerate(sides):
                got.append(send(src, to.at[h, d - 1], rs_s.at[s, h, 2, d - 1], rs_r.at[s, h, 2, d - 1], who))
        return got

    def scatter_sum(s, cps, out):
        arrived(cps)
        at_a, at_b, to = ((sa, sb, r2), (sa1, sb1, r21))[s]
        for h, own in enumerate((pick_a(at_a, y), pick_b(at_b, x))):
            total = own[...].astype(F32)
            for d in range(3):
                total += to[h, d].astype(F32)
            out[:, cols_of[h]] = total.astype(out.dtype)

    gate_load.wait()
    up_load.wait()
    arrived(t0a)
    arrived(t1p)
    t1a = ag2(0, 1, 0)
    multiply(0, 0)
    multiply(1, 0)
    t1b = ag2(0, 1, 1)
    pair_sum(0, 0)
    pair_sum(1, 0)
    arrived([og_hop])
    o1p = ag1(1, 1)
    arrived(t1a)
    multiply(0, 2)
    arrived(o1p)
    o1a = ag2(1, 1, 0)
    multiply(1, 2)
    o0p = ag1(1, 0, ogown)
    pair_sum(0, 2)
    pair_sum(1, 2)
    o1b = ag2(1, 1, 1)
    arrived(t1b)
    multiply(0, 3)
    multiply(1, 3)
    arrived(o0p)
    o0a = ag2(1, 0, 0)
    pair_sum(0, 3)
    pair_sum(1, 3)
    t0b = ag2(0, 0, 1)
    down_load.wait()
    arrived(o1a)
    multiply(2, 2)
    o0b = ag2(1, 0, 1)
    hid0 = activate(0)
    pair_sum(2, 2)
    arrived(o1b)
    multiply(2, 3)
    hid2 = activate(2)
    pair_sum(2, 3)
    arrived(o0a)
    multiply(2, 0)
    arrived(t0b)
    multiply(0, 1)
    pair_sum(2, 0)
    multiply(1, 1)
    pair_sum(0, 1)
    pair_sum(1, 1)
    hid3 = activate(3)
    k2 = act_grad(2)
    k3 = act_grad(3)
    arrived(o0b)
    multiply(2, 1)
    pair_sum(2, 1)
    later = []
    g23 = grad_in((2, 3), (k2, k3), lambda: later.append(act_grad(0)))
    g0 = grad_in((0,), later, lambda: later.append(activate(1)))
    k1 = act_grad(1)
    arrived([hid0, later[1], hid2, hid3])

    def down_tile(i, carry):
        rows = pl.ds(pl.multiple_of(i * 128, 128), 128)
        value = dot(hid[:, rows], og[...].reshape(TOKENS, WIDTH), ((0,), (0,)))
        gdown_ref[rows, :] = value.astype(BF16)
        return carry

    lax.fori_loop(0, 4, down_tile, 0)
    p1 = []

    def between():
        first_sum(1, 0, g23[0::2])
        first_sum(1, 1, g23[1::2])
        p1.extend(scatter2(1))

    g1 = grad_in((1,), (k1,), between)

    def gate_tile(i, carry):
        rows = pl.ds(pl.multiple_of(i * 256, 256), 256)
        left = tok[:, :, :, :, :, :, rows].reshape(TOKENS, 256)
        value = dot(left, jnp.concatenate([gug[0], gug[1]], axis=1), ((0,), (0,)))
        ggate_ref[rows, :] = value[:, :UNITS].astype(BF16)
        gup_ref[rows, :] = value[:, UNITS:].astype(BF16)
        return carry

    first_sum(0, 0, g0)
    lax.fori_loop(0, 5, gate_tile, 0)
    first_sum(0, 1, g1)
    p0 = scatter2(0)
    scatter_sum(1, p1, hsrc)
    last = send(hsrc, hdst, f_s.at[0], f_r.at[0], at_zh)
    lax.fori_loop(5, 8, gate_tile, 0)
    lax.fori_loop(4, UNITS // 128, down_tile, 0)
    scatter_sum(0, p0, fin)
    last.wait_recv()
    gin_ref[...] = (fin[...] + hdst[...].astype(F32)).astype(BF16)
    for cp in sent:
        cp.wait_send()


def on_device(tokens, cotangent, gate_weight, up_weight, down_weight, seq_ids, chosen, margins, counts):
    vmem = pl.BlockSpec(memory_space=pltpu.VMEM)
    smem = pl.BlockSpec(memory_space=pltpu.SMEM)
    hbm = pl.BlockSpec(memory_space=pl.ANY)
    dma = pltpu.SemaphoreType.DMA
    results = pl.pallas_call(
        kernel,
        out_shape=(
            pltpu.VMEM((ROWS, WIDTH), BF16),
            pltpu.VMEM((WIDTH, UNITS), BF16),
            pltpu.VMEM((WIDTH, UNITS), BF16),
            pltpu.VMEM((UNITS, WIDTH), BF16),
        ),
        in_specs=[hbm, hbm, hbm, hbm, hbm, smem, smem, smem, smem],
        out_specs=(vmem, vmem, vmem, vmem),
        scratch_shapes=[
            pltpu.VMEM((WIDTH, UNITS), BF16),
            pltpu.VMEM((WIDTH, UNITS), BF16),
            pltpu.VMEM((UNITS, WIDTH), BF16),
            pltpu.VMEM((2, 2, 2, 2, 2, ROWS, WIDTH), BF16),
            pltpu.VMEM((2, 2, 2, 2, 2, ROWS, WIDTH), BF16),
            pltpu.VMEM((ROWS, WIDTH), BF16),
            pltpu.VMEM((ROWS, WIDTH), BF16),
            pltpu.VMEM((3, TOKENS, UNITS), F32),
            pltpu.VMEM((3, 256, UNITS), BF16),
            pltpu.VMEM((3, 256, UNITS), BF16),
            pltpu.VMEM((3, 256, UNITS), F32),
            pltpu.VMEM((3, 256, UNITS), BF16),
            pltpu.VMEM((3, 256, UNITS), BF16),
            pltpu.VMEM((256, UNITS), F32),
            pltpu.VMEM((256, UNITS), F32),
            pltpu.VMEM((TOKENS, UNITS), BF16),
            pltpu.VMEM((2, TOKENS, UNITS), BF16),
            pltpu.VMEM((2, 2, 2, 2, 2, ROWS, WIDTH), BF16),
            pltpu.VMEM((2, 2, 3, 2, ROWS, HALF), BF16),
            pltpu.VMEM((2, 2, 3, 2, ROWS, HALF), BF16),
            pltpu.VMEM((2, 2, ROWS, HALF), BF16),
            pltpu.VMEM((2, 2, ROWS, HALF), BF16),
            pltpu.VMEM((2, 3, ROWS, HALF), BF16),
            pltpu.VMEM((2, 2, ROWS, HALF), BF16),
            pltpu.VMEM((2, 2, ROWS, HALF), BF16),
            pltpu.VMEM((2, 3, ROWS, HALF), BF16),
            pltpu.VMEM((ROWS, WIDTH), F32),
            pltpu.VMEM((ROWS, WIDTH), BF16),
            pltpu.VMEM((ROWS, WIDTH), BF16),
            dma((5,)),
            dma((2,)),
            dma((2,)),
            dma((2, 2, 2, 3, 3)),
            dma((2, 2, 2, 3, 3)),
            dma((4, 3)),
            dma((4, 3)),
            dma((4, 3)),
            dma((4, 3)),
            dma((4,)),
            dma((4,)),
            dma((4,)),
            dma((4,)),
            dma((2, 2, 3, 3)),
            dma((2, 2, 3, 3)),
            dma((1,)),
            dma((1,)),
        ],
        compiler_params=pltpu.CompilerParams(
            collective_id=0, has_side_effects=True, vmem_limit_bytes=46 << 20
        ),
        cost_estimate=pl.CostEstimate(flops=15_000_000_000, bytes_accessed=22_000_000, transcendentals=0),
        name="simpo_backward",
    )(tokens, cotangent, gate_weight, up_weight, down_weight, seq_ids, chosen, margins, counts)
    return write_out(*results)


def write_out(*grads):
    count = len(grads)

    def body(*refs):
        sem = refs[-1]
        copies = [pltpu.make_async_copy(refs[i], refs[count + i], sem.at[i]) for i in range(count)]
        for cp in copies:
            cp.start()
        for cp in copies:
            cp.wait()

    return pl.pallas_call(
        body,
        out_shape=tuple(jax.ShapeDtypeStruct(g.shape, g.dtype) for g in grads),
        in_specs=[pl.BlockSpec(memory_space=pltpu.VMEM)] * count,
        out_specs=(pl.BlockSpec(memory_space=pl.ANY),) * count,
        scratch_shapes=[pltpu.SemaphoreType.DMA((count,))],
        compiler_params=pltpu.CompilerParams(vmem_limit_bytes=1 << 20),
        name="write_out",
    )(*grads)


def solution(mesh):
    return jax.shard_map(
        on_device,
        mesh=mesh,
        in_specs=(
            P(("out", "dep"), "inp"),
            P(("out", "dep"), "inp"),
            P("inp", ("out", "dep")),
            P("inp", ("out", "dep")),
            P(("out", "dep"), "inp"),
            P(("out", "dep")),
            P(("out", "dep")),
            P(),
            P(),
        ),
        out_specs=(
            P(("out", "dep"), "inp"),
            P("inp", ("out", "dep")),
            P("inp", ("out", "dep")),
            P(("out", "dep"), "inp"),
        ),
        check_vma=False,
    )
```
